32 devices in a mesh: grp: 8 (over z, y), tp: 4 (over x, core).
Axes of the slice: x: 2, y: 2, z: 4, core: 2. Of those that a mesh axis runs over, the one named last changes fastest.
Arguments:
- tokens: bfloat16 [2048, 2048], P('grp', 'tp'), may hold values from -6 to 6
- attn_gain: float32 [2048], replicated, may hold values from 0.6 to 6
- w_query: bfloat16 [2048, 2048], P(None, 'tp'), may hold values from -0.125 to 0.125
- w_key: bfloat16 [2048, 512], P(None, 'tp'), may hold values from -0.125 to 0.125
- w_value: bfloat16 [2048, 512], P(None, 'tp'), may hold values from -0.125 to 0.125
- w_out: bfloat16 [2048, 2048], P('tp'), may hold values from -0.125 to 0.125
- mlp_gain: float32 [2048], replicated, may hold values from 0.1 to 1.9
- w_gate: bfloat16 [2048, 4096], P('grp', 'tp'), may hold values from -0.125 to 0.125
- w_up: bfloat16 [2048, 4096], P('grp', 'tp'), may hold values from -0.125 to 0.125
- w_down: bfloat16 [4096, 2048], P('tp', 'grp'), may hold values from -0.09375 to 0.09375
- k_cache: bfloat16 [8, 16384, 512], P(None, 'grp', 'tp'), may hold values from -72 to 72
- v_cache: bfloat16 [8, 16384, 512], P(None, 'grp', 'tp'), may hold values from -6 to 6
- prefix_len: int32 [8], replicated, may hold values from 0 to 16128, as said below
Outputs:
- result: float32 [2048, 2048], P('grp', 'tp')
- k_cache_out: bfloat16 [8, 16384, 512], P(None, 'grp', 'tp')
- v_cache_out: bfloat16 [8, 16384, 512], P(None, 'grp', 'tp')
The draws below stay inside these ranges and needn't reach their ends.
Inputs may be any that keep to these rules, and one draw needn't show every extreme that they name: `prefix_len`: some request has none cached and some has 16128.
All inputs are finite; a program needn't handle non-finite values.
Results may differ from the reference program's by a relative error of at most 0.04.
Values may be sent and summed in bfloat16 or wider, within the bound.
No kernel may reach another device: no remote copies, remote signals or barrier semaphores. Data moves between devices by JAX's collectives and lax.ppermute only.
A program may use at most 448 MiB of HBM per device.

```python
import jax
import jax.numpy as jnp
from jax import lax

D = 2048
HEADS = 32
KVH = 8
HD = 64
FF = 4096
NEW_TOK = 256
CTX = 16384
REQ = 8
TOKENS = 2048
N_GRP = 8


def draw_attn_gain(key, part):
    return jax.random.uniform(jax.random.fold_in(key, 12), (D,), jnp.float32, 0.6, 1.4)


def draw_k_cache(key, part):
    base = jnp.clip(jax.random.normal(jax.random.fold_in(key, 21), (REQ, CTX, KVH * HD), jnp.float32), -6.0, 6.0)
    return base.astype(jnp.bfloat16)


def draw_prefix_len(key, part):
    lengths = jax.random.randint(jax.random.fold_in(key, 31), (REQ,), 0, CTX - NEW_TOK + 1, dtype=jnp.int32)
    order = jax.random.permutation(jax.random.fold_in(key, 32), REQ)
    lengths = lengths.at[order[0]].set(CTX - NEW_TOK)
    lengths = lengths.at[order[1]].set(0)
    return lengths


def block_levels(stream_key, shape, split, low, high):
    factor_of = 1.0
    for dim, blocks in split:
        steps = jax.random.uniform(jax.random.fold_in(jax.random.fold_in(stream_key, 6), dim), (blocks,), jnp.float32, low / len(split), high / len(split))
        factor_of = factor_of * jnp.repeat(jnp.exp(steps), shape[dim] // blocks).reshape((-1,) + (1,) * (len(shape) - 1 - dim))
    return factor_of


def gaussian(stream_key, extent, spread, most, split=(), kind=jnp.bfloat16):
    array = spread * jax.random.normal(stream_key, extent, jnp.float32)
    if split:
        array = array * block_levels(stream_key, extent, split, -0.22, 0.18)
    return jnp.clip(array, -most, most).astype(kind)


def setup_inputs(seed: int = 0) -> dict:
    seeds = jax.random.split(jax.random.key(seed), 14)
    tokens = gaussian(seeds[0], (TOKENS, D), 1.0, 6.0, ((0, 8), (1, 4)))
    attn_gain = draw_attn_gain(jax.random.fold_in(seeds[13], 71), 0)
    w_query = gaussian(seeds[2], (D, HEADS * HD), D ** -0.5, 0.125, ((1, 4),))
    w_key = gaussian(seeds[3], (D, KVH * HD), D ** -0.5, 0.125, ((1, 4),))
    w_value = gaussian(seeds[4], (D, KVH * HD), D ** -0.5, 0.125, ((1, 4),))
    w_out = gaussian(seeds[5], (HEADS * HD, D), (HEADS * HD) ** -0.5, 0.125, ((0, 4),))
    mlp_gain = jnp.clip(1.0 + 0.18 * jax.random.normal(seeds[6], (D,), jnp.float32), 0.1, 1.9)
    w_gate = gaussian(seeds[7], (D, FF), D ** -0.5, 0.125, ((0, 8), (1, 4)))
    w_up = gaussian(seeds[8], (D, FF), D ** -0.5, 0.125, ((0, 8), (1, 4)))
    w_down = gaussian(seeds[9], (FF, D), FF ** -0.5, 0.09375, ((0, 4), (1, 8)))
    k_cache = draw_k_cache(jax.random.fold_in(seeds[13], 71), 0)
    v_cache = gaussian(seeds[11], (REQ, CTX, KVH * HD), 1.0, 6.0, ((1, 8), (2, 4)))
    prefix_len = draw_prefix_len(jax.random.fold_in(seeds[13], 71), 0)
    return dict(tokens=tokens, attn_gain=attn_gain, w_query=w_query, w_key=w_key, w_value=w_value, w_out=w_out, mlp_gain=mlp_gain, w_gate=w_gate, w_up=w_up, w_down=w_down, k_cache=k_cache, v_cache=v_cache, prefix_len=prefix_len)


eps_norm = 1e-05
rope_base = 500000.0
neg_fill = -1e+30

def rms_scale(rows, gain):
    rows = rows.astype(jnp.float32)
    return rows * lax.rsqrt(lax.optimization_barrier(jnp.mean(rows * rows, axis=-1, keepdims=True)) + eps_norm) * gain.astype(jnp.float32)

def rotate(heads, positions):
    width = heads.shape[-1]
    half = width // 2
    inverse = rope_base ** (-2.0 * jnp.arange(half, dtype=jnp.float32) / width)
    angles = positions.astype(jnp.float32)[:, None] * inverse[None, :]
    cosine = jnp.cos(angles)[:, None, :]
    sine = jnp.sin(angles)[:, None, :]
    first = heads[..., :half]
    second = heads[..., half:]
    return jnp.concatenate([first * cosine - second * sine, second * cosine + first * sine], axis=-1)

def shard_partial(query, keys, values, start, plen):
    scores = jnp.einsum('tkgd,skd->kgts', query.astype(jnp.float32), keys.astype(jnp.float32)) * 0.125
    live = start + jnp.arange(keys.shape[0], dtype=jnp.int32) < plen
    masked = jnp.where(live, scores, neg_fill)
    top = lax.optimization_barrier(jnp.max(masked, axis=-1))
    expo = jnp.where(live, jnp.exp(masked - top[..., None]), 0.0)
    total = lax.optimization_barrier(jnp.sum(expo, axis=-1))
    weights = expo.astype(jnp.bfloat16)
    summed = jnp.einsum('kgts,skd->tkgd', weights.astype(jnp.float32), values.astype(jnp.float32))
    total_t = jnp.transpose(total, (2, 0, 1))
    scaled = summed / jnp.maximum(total_t, 1.0)[..., None]
    return (scaled.astype(jnp.bfloat16), jnp.transpose(top, (2, 0, 1)), total_t)

def fresh_partial(query, keys, values):
    scores = jnp.einsum('tkgd,ukd->kgtu', query.astype(jnp.float32), keys.astype(jnp.float32)) * 0.125
    count = keys.shape[0]
    causal = jnp.arange(count, dtype=jnp.int32)[:, None] >= jnp.arange(count, dtype=jnp.int32)[None, :]
    masked = jnp.where(causal, scores, neg_fill)
    top = lax.optimization_barrier(jnp.max(masked, axis=-1))
    expo = jnp.where(causal, jnp.exp(masked - top[..., None]), 0.0)
    total = lax.optimization_barrier(jnp.sum(expo, axis=-1))
    weights = expo.astype(jnp.bfloat16)
    summed = jnp.einsum('kgtu,ukd->tkgd', weights.astype(jnp.float32), values.astype(jnp.float32))
    total_t = jnp.transpose(total, (2, 0, 1))
    return (summed / total_t[..., None], jnp.transpose(top, (2, 0, 1)), total_t)

def merge_parts(own_out, own_top, own_total, shard_out, shard_top, shard_total):
    peak = jnp.maximum(own_top, lax.optimization_barrier(jnp.max(shard_top, axis=0)))
    own_weight = jnp.exp(own_top - peak) * own_total
    shard_weight = jnp.exp(shard_top - peak[None]) * shard_total
    numer = own_weight[..., None] * own_out + lax.optimization_barrier(jnp.sum(shard_weight[..., None] * shard_out.astype(jnp.float32), axis=0))
    return numer / (own_weight + lax.optimization_barrier(jnp.sum(shard_weight, axis=0)))[..., None]

def request_attention(items):
    query, key_new, value_new, key_old, value_old, plen = items
    groups = HEADS // KVH
    query = query.reshape(NEW_TOK, KVH, groups, HD)
    key_new = key_new.reshape(NEW_TOK, KVH, HD)
    value_new = value_new.reshape(NEW_TOK, KVH, HD)
    span = CTX // N_GRP
    key_old = key_old.reshape(N_GRP, span, KVH, HD)
    value_old = value_old.reshape(N_GRP, span, KVH, HD)
    starts = jnp.arange(N_GRP, dtype=jnp.int32) * span
    shard_out, shard_top, shard_total = jax.vmap(shard_partial, in_axes=(None, 0, 0, 0, None))(query, key_old, value_old, starts, plen)
    own_out, own_top, own_total = fresh_partial(query, key_new, value_new)
    merged = merge_parts(own_out, own_top, own_total, shard_out, shard_top, shard_total)
    return merged.reshape(NEW_TOK, HEADS * HD).astype(jnp.bfloat16)

def append_rows(cache, rows, plen):
    return lax.dynamic_update_slice_in_dim(cache, rows, plen, 0)

def reference(tokens, attn_gain, w_query, w_key, w_value, w_out, mlp_gain, w_gate, w_up, w_down, k_cache, v_cache, prefix_len):
    normed = rms_scale(tokens, attn_gain).astype(jnp.bfloat16)
    positions = prefix_len[:, None] + jnp.arange(NEW_TOK, dtype=jnp.int32)[None, :]
    query = jnp.dot(normed, w_query, preferred_element_type=jnp.float32).reshape(REQ, NEW_TOK, HEADS, HD)
    query = jax.vmap(rotate)(query, positions).astype(jnp.bfloat16)
    key_new = jnp.dot(normed, w_key, preferred_element_type=jnp.float32).reshape(REQ, NEW_TOK, KVH, HD)
    key_new = jax.vmap(rotate)(key_new, positions).astype(jnp.bfloat16).reshape(REQ, NEW_TOK, KVH * HD)
    value_new = jnp.dot(normed, w_value, preferred_element_type=jnp.float32).astype(jnp.bfloat16).reshape(REQ, NEW_TOK, KVH * HD)
    attended = lax.map(request_attention, (query.reshape(REQ, NEW_TOK, HEADS * HD), key_new, value_new, k_cache, v_cache, prefix_len))
    attended = attended.reshape(TOKENS, HEADS * HD)
    first = (tokens.astype(jnp.float32) + jnp.dot(attended, w_out, preferred_element_type=jnp.float32)).astype(jnp.bfloat16)
    normed_two = rms_scale(first, mlp_gain).astype(jnp.bfloat16)
    gate = jnp.dot(normed_two, w_gate, preferred_element_type=jnp.float32)
    upward = jnp.dot(normed_two, w_up, preferred_element_type=jnp.float32)
    hidden = (jax.nn.silu(gate) * upward).astype(jnp.bfloat16)
    result = first.astype(jnp.float32) + jnp.dot(hidden, w_down, preferred_element_type=jnp.float32)
    k_cache_out = jax.vmap(append_rows)(k_cache, key_new, prefix_len)
    v_cache_out = jax.vmap(append_rows)(v_cache, value_new, prefix_len)
    return (result, k_cache_out, v_cache_out)
```

```python
import functools

import jax
import jax.numpy as jnp
from jax import lax
from jax.experimental import pallas as pl
from jax.experimental.pallas import tpu as pltpu
from jax.sharding import PartitionSpec as P

HD = 64
NEW_TOK = 256
PER_KV = 4
HALF = PER_KV * HD
PAY = HALF + 16

eps_norm = 1e-05
rope_base = 500000.0
neg_fill = -1e30

f32 = jnp.float32
bf16 = jnp.bfloat16

VMEM_BIG = 56 << 20


def params(limit=VMEM_BIG):
    return pltpu.CompilerParams(vmem_limit_bytes=limit)


def whole_spec():
    return pl.BlockSpec(memory_space=pltpu.VMEM)


def project_kernel(t_ref, x0, x1, x2, x3, gain, wq, wk, wv, cos, sin, qa, qb, k_out, v_out):
    t = t_ref[0]
    pieces = [x[...].astype(f32) for x in (x0, x1, x2, x3)]
    width = sum(x.shape[1] for x in pieces)
    total = sum(jnp.sum(x * x, axis=-1, keepdims=True) for x in pieces)
    scale = lax.rsqrt(total / width + eps_norm)
    q = k = v = 0.0
    for i, x in enumerate(pieces):
        s = t ^ i
        n = (x * scale * gain[s]).astype(bf16)
        q += jnp.dot(n, wq[s], preferred_element_type=f32)
        k += jnp.dot(n, wk[s], preferred_element_type=f32)
        v += jnp.dot(n, wv[s], preferred_element_type=f32)
    c, s = cos[...], sin[...]

    def rotate(cols):
        a, b = cols[: HD // 2], cols[HD // 2 :]
        return [a * c - b * s, b * c + a * s]

    qt = q.T
    rows = []
    for h in range(qt.shape[0] // HD):
        rows += rotate(qt[h * HD : (h + 1) * HD])
    turned = (jnp.concatenate(rows, axis=0).astype(bf16) * 0.125).astype(bf16)
    qa[...] = turned[:HALF]
    qb[...] = turned[HALF:]
    kt = k.T
    rows = []
    for h in range(kt.shape[0] // HD):
        rows += rotate(kt[h * HD : (h + 1) * HD])
    k_out[...] = jnp.concatenate(rows, axis=0).T.astype(bf16)
    v_out[...] = v.astype(bf16)


def project(t, pieces, gain, w_query, w_key, w_value, cos, sin):
    tp = len(pieces)
    part = pieces[0].shape[1]
    smem = pl.BlockSpec(memory_space=pltpu.SMEM)
    return pl.pallas_call(
        project_kernel,
        in_specs=[smem] + [whole_spec()] * 10,
        out_specs=[whole_spec()] * 4,
        out_shape=[
            jax.ShapeDtypeStruct((HALF, NEW_TOK), bf16),
            jax.ShapeDtypeStruct((HALF, NEW_TOK), bf16),
            jax.ShapeDtypeStruct((NEW_TOK, w_key.shape[1]), bf16),
            jax.ShapeDtypeStruct((NEW_TOK, w_value.shape[1]), bf16),
        ],
        compiler_params=params(),
        cost_estimate=pl.CostEstimate(flops=2 * 10**9, bytes_accessed=4 << 20, transcendentals=0),
        name="project",
    )(
        t,
        *pieces,
        gain.reshape(tp, 1, part),
        w_query.reshape(tp, part, -1),
        w_key.reshape(tp, part, -1),
        w_value.reshape(tp, part, -1),
        cos,
        sin,
    )


def attend_item(q, kv, live, k_ref, v_ref, o_ref, s_ref, vt_ref):
    span = k_ref.shape[1]
    chunk = min(512, span)
    chunks = span // chunk
    zero = jnp.zeros((HD, NEW_TOK), bf16)
    ones = jnp.ones((16, span), bf16)

    def run(masked):
        vt_ref[...] = v_ref[0].T
        values = jnp.concatenate([vt_ref[pl.ds(pl.multiple_of(kv * HD, HD), HD), :], ones], axis=0)
        first_kv = kv == 0

        def scores(h):
            own = q[h * HD : (h + 1) * HD]
            wide = jnp.concatenate([jnp.where(first_kv, own, zero), jnp.where(first_kv, zero, own)], axis=0)
            top = None
            for c in range(chunks):
                s = jnp.dot(k_ref[0, c * chunk : (c + 1) * chunk, :], wide, preferred_element_type=f32)
                if masked:
                    at = lax.broadcasted_iota(jnp.int32, s.shape, 0) + c * chunk
                    s = jnp.where(at < live, s, neg_fill)
                s_ref[h % 2, c * chunk : (c + 1) * chunk, :] = s
                here = jnp.max(s, axis=0, keepdims=True)
                top = here if top is None else jnp.maximum(top, here)
            return top

        top = scores(0)
        logs = []
        for h in range(PER_KV):
            later = scores(h + 1) if h + 1 < PER_KV else None
            acc = jnp.zeros((HD + 16, NEW_TOK), f32)
            for c in range(chunks):
                s = s_ref[h % 2, c * chunk : (c + 1) * chunk, :]
                p = jnp.exp(s - top).astype(bf16)
                acc = acc + jnp.dot(values[:, c * chunk : (c + 1) * chunk], p, preferred_element_type=f32)
            total = acc[HD : HD + 1]
            o_ref[h * HD : (h + 1) * HD, :] = (acc[:HD] / total).astype(bf16)
            logs.append(top + jnp.log(total))
            top = later
        put_logs(jnp.concatenate(logs, axis=0), o_ref)

    pl.when(live >= span)(lambda: run(False))
    pl.when((live > 0) & (live < span))(lambda: run(True))

    @pl.when(live <= 0)
    def _():
        o_ref[:HALF, :] = jnp.zeros((HALF, NEW_TOK), bf16)
        put_logs(jnp.full((PER_KV, NEW_TOK), neg_fill, f32), o_ref)


def put_logs(logs, o_ref):
    high = logs.astype(bf16).astype(f32)
    rest = logs - high
    middle = rest.astype(bf16).astype(f32)
    low = rest - middle
    rows = jnp.concatenate([high, middle, low, jnp.zeros_like(low)], axis=0)
    o_ref[HALF:, :] = rows.astype(bf16)


def get_logs(rows):
    rows = rows.astype(f32)
    return rows[:PER_KV] + rows[PER_KV : 2 * PER_KV] + rows[2 * PER_KV : 3 * PER_KV]


def attend_pair_kernel(req, live, qa, qb, k_ref, v_ref, oa, ob, s_ref, vt_ref):
    i = pl.program_id(0)

    @pl.when(i == 0)
    def _():
        attend_item(qa[...], 0, live[0], k_ref, v_ref, oa, s_ref, vt_ref)

    @pl.when(i == 1)
    def _():
        attend_item(qb[...], 1, live[1], k_ref, v_ref, ob, s_ref, vt_ref)


def attend_pair(req, live, qa, qb, k_cache, v_cache):
    span, width = k_cache.shape[1:]
    cache = pl.BlockSpec((1, span, width), lambda i, req, live: (req[i], 0, 0))
    query = pl.BlockSpec((HALF, NEW_TOK), lambda i, req, live: (0, 0))
    out = pl.BlockSpec((PAY, NEW_TOK), lambda i, req, live: (0, 0))
    return pl.pallas_call(
        attend_pair_kernel,
        grid_spec=pltpu.PrefetchScalarGridSpec(
            num_scalar_prefetch=2,
            grid=(2,),
            in_specs=[query, query, cache, cache],
            out_specs=[out, out],
            scratch_shapes=[pltpu.VMEM((2, span, NEW_TOK), f32), pltpu.VMEM((width, span), bf16)],
        ),
        out_shape=[jax.ShapeDtypeStruct((PAY, NEW_TOK), bf16)] * 2,
        compiler_params=params(),
        cost_estimate=pl.CostEstimate(flops=6 * 10**9, bytes_accessed=4 << 20, transcendentals=1 << 22),
        name="attend",
    )(req, live, qa, qb, k_cache, v_cache)


def attend_all_kernel(live, q_ref, k_ref, v_ref, o_ref, s_ref, vt_ref):
    attend_item(q_ref[0], pl.program_id(1), live[pl.program_id(0)], k_ref, v_ref, o_ref.at[0], s_ref, vt_ref)


def attend_all(live, query, k_cache, v_cache):
    requests, span, width = k_cache.shape
    cache = pl.BlockSpec((1, span, width), lambda r, j, live: (r, 0, 0))
    return pl.pallas_call(
        attend_all_kernel,
        grid_spec=pltpu.PrefetchScalarGridSpec(
            num_scalar_prefetch=1,
            grid=(requests, 2),
            in_specs=[pl.BlockSpec((1, HALF, NEW_TOK), lambda r, j, live: (r, j, 0)), cache, cache],
            out_specs=pl.BlockSpec((1, PAY, NEW_TOK), lambda r, j, live: (r, j, 0)),
            scratch_shapes=[pltpu.VMEM((2, span, NEW_TOK), f32), pltpu.VMEM((width, span), bf16)],
        ),
        out_shape=jax.ShapeDtypeStruct((requests, 2 * PAY, NEW_TOK), bf16),
        compiler_params=params(),
        name="attend",
    )(live, query, k_cache, v_cache)


def fresh_kernel(qa, qb, k_ref, v_ref, o_ref, l_ref):
    zero = jnp.zeros((HD, NEW_TOK), bf16)
    ones = jnp.ones((16, NEW_TOK), bf16)
    vt = v_ref[...].T
    at = lax.broadcasted_iota(jnp.int32, (NEW_TOK, NEW_TOK), 0)
    token = lax.broadcasted_iota(jnp.int32, (NEW_TOK, NEW_TOK), 1)
    causal = at <= token
    logs = []
    for h in range(2 * PER_KV):
        j = h // PER_KV
        own = (qa, qb)[j][(h % PER_KV) * HD : (h % PER_KV + 1) * HD, :]
        wide = jnp.concatenate([own, zero] if j == 0 else [zero, own], axis=0)
        s = jnp.dot(k_ref[...], wide, preferred_element_type=f32)
        s = jnp.where(causal, s, neg_fill)
        top = jnp.max(s, axis=0, keepdims=True)
        p = jnp.where(causal, jnp.exp(s - top), 0.0).astype(bf16)
        values = jnp.concatenate([vt[j * HD : (j + 1) * HD], ones], axis=0)
        acc = jnp.dot(values, p, preferred_element_type=f32)
        total = acc[HD : HD + 1]
        o_ref[h * HD : (h + 1) * HD, :] = acc[:HD] / total
        logs.append(top + jnp.log(total))
    l_ref[...] = jnp.concatenate(logs, axis=0)


def fresh(qa, qb, key_new, value_new):
    return pl.pallas_call(
        fresh_kernel,
        in_specs=[whole_spec()] * 4,
        out_specs=[whole_spec()] * 2,
        out_shape=[
            jax.ShapeDtypeStruct((2 * HALF, NEW_TOK), f32),
            jax.ShapeDtypeStruct((2 * PER_KV, NEW_TOK), f32),
        ],
        compiler_params=params(),
        cost_estimate=pl.CostEstimate(flops=2 * 10**9, bytes_accessed=2 << 20, transcendentals=1 << 19),
        name="fresh",
    )(qa, qb, key_new, value_new)


def append_kernel(offset, new_k, new_v, k_ref, v_ref, k_out, v_out):
    off = offset[pl.program_id(0)]
    span = k_ref.shape[1]
    window = NEW_TOK + 16
    k_out[...] = k_ref[...]
    v_out[...] = v_ref[...]

    @pl.when((off > -NEW_TOK) & (off < span))
    def _():
        at = pl.multiple_of(jnp.clip(off // 16 * 16, 0, span - window), 16)
        row = lax.broadcasted_iota(jnp.int32, (window, NEW_TOK), 0) + (at - off)
        pick = (row == lax.broadcasted_iota(jnp.int32, (window, NEW_TOK), 1)).astype(bf16)
        width = k_ref.shape[2]
        inside = lax.broadcasted_iota(jnp.int32, (window, width), 0) + (at - off)
        inside = (inside >= 0) & (inside < NEW_TOK)
        for new, old, out in ((new_k, k_ref, k_out), (new_v, v_ref, v_out)):
            rows = jnp.dot(pick, new[0], preferred_element_type=f32)
            kept = old[0, pl.ds(at, window), :].astype(f32)
            out[0, pl.ds(at, window), :] = jnp.where(inside, rows, kept).astype(bf16)


def append(offset, new_keys, new_values, k_cache, v_cache):
    requests, span, width = k_cache.shape
    cache = pl.BlockSpec((1, span, width), lambda r, off: (r, 0, 0))
    new = pl.BlockSpec((1, NEW_TOK, width), lambda r, off: (r, 0, 0))
    return pl.pallas_call(
        append_kernel,
        grid_spec=pltpu.PrefetchScalarGridSpec(
            num_scalar_prefetch=1,
            grid=(requests,),
            in_specs=[new, new, cache, cache],
            out_specs=[cache, cache],
        ),
        out_shape=[jax.ShapeDtypeStruct(k_cache.shape, bf16)] * 2,
        compiler_params=params(),
        cost_estimate=pl.CostEstimate(flops=10**9, bytes_accessed=20 << 20, transcendentals=0),
        name="append",
    )(offset, new_keys, new_values, k_cache, v_cache)


def merge_kernel(n, t_ref, *refs):
    parts = refs[: 2 * n]
    own, own_log, w_ref, send, keep, att = refs[2 * n :]
    step = pl.program_id(0)

    @pl.when(step == 0)
    def _():
        for j in range(2):
            half = parts[j * n : (j + 1) * n]
            logs = [get_logs(p[HALF:, :]) for p in half]
            mine = own_log[j * PER_KV : (j + 1) * PER_KV, :]
            peak = functools.reduce(jnp.maximum, logs, mine)
            shares = [jnp.exp(x - peak) for x in logs]
            here = jnp.exp(mine - peak)
            inverse = 1.0 / (here + sum(shares))
            for h in range(PER_KV):
                lo = j * HALF + h * HD
                numer = here[h : h + 1] * own[lo : lo + HD, :]
                for p, share in zip(half, shares):
                    numer += share[h : h + 1] * p[h * HD : (h + 1) * HD, :].astype(f32)
                att[:, lo : lo + HD] = (numer * inverse[h : h + 1]).T.astype(bf16)

    out = jnp.dot(att[...], w_ref[...], preferred_element_type=f32)

    @pl.when(step < 2)
    def _():
        send[jnp.minimum(step, 1)] = out.astype(bf16)

    @pl.when(step >= 2)
    def _():
        keep[jnp.maximum(step - 2, 0)] = out


def place_of(step, t):
    return t ^ jnp.where(step < 2, 2 * step + 1, 2 * step - 4)


def merge(t, parts_a, parts_b, own, own_log, w_out):
    n = len(parts_a)
    rows, features = w_out.shape
    part = features // 4
    pay = pl.BlockSpec((PAY, NEW_TOK), lambda s, t: (0, 0))
    shares = pl.BlockSpec((2, NEW_TOK, part), lambda s, t: (0, 0, 0))
    return pl.pallas_call(
        functools.partial(merge_kernel, n),
        grid_spec=pltpu.PrefetchScalarGridSpec(
            num_scalar_prefetch=1,
            grid=(4,),
            in_specs=[pay] * (2 * n)
            + [
                pl.BlockSpec(own.shape, lambda s, t: (0, 0)),
                pl.BlockSpec(own_log.shape, lambda s, t: (0, 0)),
                pl.BlockSpec((rows, part), lambda s, t: (0, place_of(s, t[0]))),
            ],
            out_specs=[shares, shares],
            scratch_shapes=[pltpu.VMEM((NEW_TOK, 2 * HALF), bf16)],
        ),
        out_shape=[
            jax.ShapeDtypeStruct((2, NEW_TOK, part), bf16),
            jax.ShapeDtypeStruct((2, NEW_TOK, part), f32),
        ],
        compiler_params=params(),
        cost_estimate=pl.CostEstimate(flops=2 * 10**9, bytes_accessed=8 << 20, transcendentals=0),
        name="merge",
    )(t, *parts_a, *parts_b, own, own_log, w_out)


def mlp_kernel(t_ref, x0, x1, x2, x3, gain, wg, wu, wd, send, keep, normed, hidden):
    step = pl.program_id(0)
    t = t_ref[0]
    tile = wg.shape[2]

    @pl.when(step == 0)
    def _():
        pieces = [x[...].astype(f32) for x in (x0, x1, x2, x3)]
        width = sum(x.shape[1] for x in pieces)
        total = sum(jnp.sum(x * x, axis=-1, keepdims=True) for x in pieces)
        scale = lax.rsqrt(total / width + eps_norm)
        for i, x in enumerate(pieces):
            normed[i] = (x * scale * gain[t ^ i]).astype(bf16)

    @pl.when(step < 4)
    def _():
        gate = up = 0.0
        for i in range(4):
            gate += jnp.dot(normed[i], wg[t ^ i], preferred_element_type=f32)
            up += jnp.dot(normed[i], wu[t ^ i], preferred_element_type=f32)
        hidden[jnp.minimum(step, 3)] = (gate / (1.0 + jnp.exp(-gate)) * up).astype(bf16)

    @pl.when(step >= 4)
    def _():
        blocks = []
        for b in range(wd.shape[0]):
            out = 0.0
            for i in range(4):
                out += jnp.dot(hidden[i], wd[b, i * tile : (i + 1) * tile, :], preferred_element_type=f32)
            blocks.append(out)
        out = jnp.concatenate(blocks, axis=1)

        @pl.when(step < 6)
        def _():
            send[jnp.clip(step - 4, 0, 1)] = out.astype(bf16)

        @pl.when(step >= 6)
        def _():
            keep[jnp.clip(step - 6, 0, 1)] = out


def mlp(t, pieces, gain, w_gate, w_up, w_down):
    part = pieces[0].shape[1]
    units = w_gate.shape[1]
    tile = units // 4
    groups, _, cols = w_down.shape
    piece = pl.BlockSpec((NEW_TOK, part), lambda s, t: (0, 0))
    up = pl.BlockSpec((4, part, tile), lambda s, t: (0, 0, jnp.minimum(s, 3)))
    down = pl.BlockSpec((groups // 4, units, cols), lambda s, t: (place_of(jnp.maximum(s - 4, 0), t[0]), 0, 0))
    shares = pl.BlockSpec((2, NEW_TOK, part), lambda s, t: (0, 0, 0))
    return pl.pallas_call(
        mlp_kernel,
        grid_spec=pltpu.PrefetchScalarGridSpec(
            num_scalar_prefetch=1,
            grid=(8,),
            in_specs=[piece] * 4 + [pl.BlockSpec((4, 1, part), lambda s, t: (0, 0, 0)), up, up, down],
            out_specs=[shares, shares],
            scratch_shapes=[pltpu.VMEM((4, NEW_TOK, part), bf16), pltpu.VMEM((4, NEW_TOK, tile), bf16)],
        ),
        out_shape=[
            jax.ShapeDtypeStruct((2, NEW_TOK, part), bf16),
            jax.ShapeDtypeStruct((2, NEW_TOK, part), f32),
        ],
        compiler_params=params(),
        cost_estimate=pl.CostEstimate(flops=4 * 10**9, bytes_accessed=14 << 20, transcendentals=1 << 18),
        name="mlp",
    )(
        t,
        *pieces,
        gain.reshape(4, 1, part),
        w_gate.reshape(4, part, units),
        w_up.reshape(4, part, units),
        w_down,
    )


def swap(x, bit, size=4):
    return lax.ppermute(x, "tp", [(i, i ^ bit) for i in range(size)])


def gather_pieces(x):
    across = swap(x, 2)
    beside = swap(x, 1)
    return [x, beside, across, swap(across, 1)]


def scatter_sum(send, keep):
    near = swap(send, 1)
    far = swap((keep[1] + near[1].astype(f32)).astype(bf16), 2)
    return keep[0] + near[0].astype(f32) + far.astype(f32)


def ring_order(groups):
    return list(range(0, groups, 2)) + list(range(groups - 1, 0, -2))


def shards(
    tokens,
    attn_gain,
    w_query,
    w_key,
    w_value,
    w_out,
    mlp_gain,
    w_gate,
    w_up,
    w_down,
    k_cache,
    v_cache,
    prefix_len,
):
    groups = lax.axis_size("grp")
    group = lax.axis_index("grp")
    t = lax.axis_index("tp").reshape(1)
    span = k_cache.shape[1]
    start = group * span

    all_gate = lax.all_gather(w_gate, "grp", axis=0, tiled=True)
    all_up = lax.all_gather(w_up, "grp", axis=0, tiled=True)
    all_down = lax.all_gather(w_down, "grp", axis=0)

    own_len = lax.dynamic_index_in_dim(prefix_len, group, keepdims=False)
    half = HD // 2
    inverse = rope_base ** (-2.0 * jnp.arange(half, dtype=f32) / HD)
    positions = own_len + jnp.arange(NEW_TOK, dtype=jnp.int32)
    angles = inverse[:, None] * positions.astype(f32)[None, :]
    qa, qb, key_new, value_new = project(
        t, gather_pieces(tokens), attn_gain, w_query, w_key, w_value, jnp.cos(angles), jnp.sin(angles)
    )

    new_keys = lax.all_gather(key_new, "grp", axis=0)
    new_values = lax.all_gather(value_new, "grp", axis=0)
    own, own_log = fresh(qa, qb, key_new, value_new)

    if groups == 8:
        ring = ring_order(groups)
        order = jnp.array(ring, jnp.int32)
        place = jnp.array([ring.index(g) for g in range(groups)], jnp.int32)[group]

        def shift(x, by):
            return lax.ppermute(x, "grp", [(ring[i], ring[(i + by) % groups]) for i in range(groups)])

        parts_a, parts_b = [], []
        now_a, now_b = qa, qb
        for k in range(groups):
            if k + 1 < groups:
                later_a, later_b = shift(now_a, 1), shift(now_b, -1)
            req = jnp.stack([order[(place - k) % groups], order[(place + k) % groups]])
            live = prefix_len[req] - start
            out_a, out_b = attend_pair(req, live, now_a, now_b, k_cache, v_cache)
            parts_a.append(shift(out_a, -k) if k else out_a)
            parts_b.append(shift(out_b, k) if k else out_b)
            now_a, now_b = later_a, later_b
    else:
        query = lax.all_gather(jnp.concatenate([qa, qb], axis=0), "grp", axis=0)
        out = attend_all(prefix_len - start, query, k_cache, v_cache)
        back = lax.all_to_all(out, "grp", split_axis=0, concat_axis=0, tiled=True)
        parts_a = [back[k, :PAY] for k in range(groups)]
        parts_b = [back[k, PAY:] for k in range(groups)]

    mixed = scatter_sum(*merge(t, parts_a, parts_b, own, own_log, w_out))
    first = (tokens.astype(f32) + mixed).astype(bf16)
    down = scatter_sum(*mlp(t, gather_pieces(first), mlp_gain, all_gate, all_up, all_down))
    result = first.astype(f32) + down
    k_next, v_next = append(prefix_len - start, new_keys, new_values, k_cache, v_cache)
    return (result, k_next, v_next)


def solution(mesh):
    placed = (
        P("grp", "tp"),
        P(),
        P(None, "tp"),
        P(None, "tp"),
        P(None, "tp"),
        P("tp", None),
        P(),
        P("grp", "tp"),
        P("grp", "tp"),
        P("tp", "grp"),
        P(None, "grp", "tp"),
        P(None, "grp", "tp"),
        P(),
    )
    return jax.shard_map(
        shards,
        mesh=mesh,
        in_specs=placed,
        out_specs=(P("grp", "tp"), P(None, "grp", "tp"), P(None, "grp", "tp")),
        check_vma=False,
    )
```

```python
import functools

import jax
import jax.numpy as jnp
from jax import lax
from jax.experimental import pallas as pl
from jax.experimental.pallas import tpu as pltpu
from jax.sharding import PartitionSpec as P

HD = 64
NEW_TOK = 256
PER_KV = 4
HEADS = 2 * PER_KV
FEAT = HEADS * HD
PAY = FEAT + 4 * HEADS

eps_norm = 1e-05
rope_base = 500000.0
neg_fill = -1e30

f32 = jnp.float32
bf16 = jnp.bfloat16

VMEM_BIG = 56 << 20


def params(limit=VMEM_BIG):
    return pltpu.CompilerParams(vmem_limit_bytes=limit)


def whole_spec():
    return pl.BlockSpec(memory_space=pltpu.VMEM)


def project_kernel(t_ref, x0, x1, x2, x3, gain, wq, wk, wv, cos, sin, q_out, k_out, v_out):
    t = t_ref[0]
    pieces = [x[...].astype(f32) for x in (x0, x1, x2, x3)]
    width = sum(x.shape[1] for x in pieces)
    total = sum(jnp.sum(x * x, axis=-1, keepdims=True) for x in pieces)
    scale = lax.rsqrt(total / width + eps_norm)
    q = k = v = 0.0
    for i, x in enumerate(pieces):
        s = t ^ i
        n = (x * scale * gain[s]).astype(bf16)
        q += jnp.dot(n, wq[s], preferred_element_type=f32)
        k += jnp.dot(n, wk[s], preferred_element_type=f32)
        v += jnp.dot(n, wv[s], preferred_element_type=f32)
    c, s = cos[...], sin[...]

    def rotate(cols):
        a, b = cols[: HD // 2], cols[HD // 2 :]
        return [a * c - b * s, b * c + a * s]

    qt = q.T
    rows = []
    for h in range(qt.shape[0] // HD):
        rows += rotate(qt[h * HD : (h + 1) * HD])
    q_out[...] = (jnp.concatenate(rows, axis=0).astype(bf16) * 0.125).astype(bf16)
    kt = k.T
    rows = []
    for h in range(kt.shape[0] // HD):
        rows += rotate(kt[h * HD : (h + 1) * HD])
    k_out[...] = jnp.concatenate(rows, axis=0).T.astype(bf16)
    v_out[...] = v.astype(bf16)


def project(t, pieces, gain, w_query, w_key, w_value, cos, sin):
    tp = len(pieces)
    part = pieces[0].shape[1]
    smem = pl.BlockSpec(memory_space=pltpu.SMEM)
    return pl.pallas_call(
        project_kernel,
        in_specs=[smem] + [whole_spec()] * 10,
        out_specs=[whole_spec()] * 3,
        out_shape=[
            jax.ShapeDtypeStruct((w_query.shape[1], NEW_TOK), bf16),
            jax.ShapeDtypeStruct((NEW_TOK, w_key.shape[1]), bf16),
            jax.ShapeDtypeStruct((NEW_TOK, w_value.shape[1]), bf16),
        ],
        compiler_params=params(),
        cost_estimate=pl.CostEstimate(flops=2 * 10**9, bytes_accessed=4 << 20, transcendentals=0),
        name="project",
    )(
        t,
        *pieces,
        gain.reshape(tp, 1, part),
        w_query.reshape(tp, part, -1),
        w_key.reshape(tp, part, -1),
        w_value.reshape(tp, part, -1),
        cos,
        sin,
    )


def put_logs(logs, o_ref):
    high = logs.astype(bf16).astype(f32)
    rest = logs - high
    middle = rest.astype(bf16).astype(f32)
    low = rest - middle
    rows = jnp.concatenate([high, middle, low, jnp.zeros_like(low)], axis=0)
    o_ref[FEAT:, :] = rows.astype(bf16)


def get_logs(rows):
    rows = rows.astype(f32)
    return rows[:HEADS] + rows[HEADS : 2 * HEADS] + rows[2 * HEADS : 3 * HEADS]


def attend_request(live, q_ref, k_ref, v_ref, fresh, o_ref, s_ref, vt_ref):
    span = k_ref.shape[1]
    chunk = min(512, span)
    zero = jnp.zeros((HD, NEW_TOK), bf16)

    def run(cached, masked):
        pieces = [(c * chunk, chunk) for c in range(span // chunk)] if cached else []
        if cached:
            vt_ref[:, :span] = v_ref[0].T
        if fresh:
            pieces.append((span, NEW_TOK))
            vt_ref[:, span:] = fresh[1][...].T

        def scores(h):
            own = q_ref[h * HD : (h + 1) * HD, :]
            wide = jnp.concatenate([own, zero] if h < PER_KV else [zero, own], axis=0)
            top = None
            for lo, rows in pieces:
                keys = k_ref[0, lo : lo + rows, :] if lo < span else fresh[0][...]
                s = jnp.dot(keys, wide, preferred_element_type=f32)
                at = lax.broadcasted_iota(jnp.int32, s.shape, 0)
                if lo >= span:
                    s = jnp.where(at <= lax.broadcasted_iota(jnp.int32, s.shape, 1), s, neg_fill)
                elif masked:
                    s = jnp.where(at < live - lo, s, neg_fill)
                s_ref[h % 2, lo : lo + rows, :] = s
                here = jnp.max(s, axis=0, keepdims=True)
                top = here if top is None else jnp.maximum(top, here)
            return top

        top = scores(0)
        logs = []
        for h in range(HEADS):
            later = scores(h + 1) if h + 1 < HEADS else None
            j = h // PER_KV
            acc = jnp.zeros((HD + 16, NEW_TOK), f32)
            for lo, rows in pieces:
                p = jnp.exp(s_ref[h % 2, lo : lo + rows, :] - top).astype(bf16)
                values = jnp.concatenate(
                    [vt_ref[j * HD : (j + 1) * HD, lo : lo + rows], jnp.ones((16, rows), bf16)], axis=0
                )
                acc = acc + jnp.dot(values, p, preferred_element_type=f32)
            total = acc[HD : HD + 1]
            o_ref[h * HD : (h + 1) * HD, :] = (acc[:HD] / total).astype(bf16)
            logs.append(top + jnp.log(total))
            top = later
        put_logs(jnp.concatenate(logs, axis=0), o_ref)

    pl.when(live >= span)(lambda: run(True, False))
    pl.when((live > 0) & (live < span))(lambda: run(True, True))

    @pl.when(live <= 0)
    def _():
        if fresh:
            run(False, False)
        else:
            o_ref[:FEAT, :] = jnp.zeros((FEAT, NEW_TOK), bf16)
            put_logs(jnp.full((HEADS, NEW_TOK), neg_fill, f32), o_ref)


def attend_kernel(call, with_new, plan, lens, q_ref, k_ref, v_ref, *refs):
    fresh, refs = (refs[:2], refs[2:]) if with_new else (None, refs)
    live = lens[plan[call]] - plan[plan.shape[0] - 1] * k_ref.shape[1]
    attend_request(live, q_ref, k_ref, v_ref, fresh, *refs)


def attend(call, plan, lens, query, k_cache, v_cache, fresh=()):
    span, width = k_cache.shape[1:]
    cache = pl.BlockSpec((1, span, width), lambda i, plan, lens: (plan[call], 0, 0))
    flat = lambda shape: pl.BlockSpec(shape, lambda i, plan, lens: (0, 0))
    long = span + (NEW_TOK if fresh else 0)
    return pl.pallas_call(
        functools.partial(attend_kernel, call, bool(fresh)),
        grid_spec=pltpu.PrefetchScalarGridSpec(
            num_scalar_prefetch=2,
            grid=(1,),
            in_specs=[flat(query.shape), cache, cache] + [flat(x.shape) for x in fresh],
            out_specs=flat((PAY, NEW_TOK)),
            scratch_shapes=[pltpu.VMEM((2, long, NEW_TOK), f32), pltpu.VMEM((width, long), bf16)],
        ),
        out_shape=jax.ShapeDtypeStruct((PAY, NEW_TOK), bf16),
        compiler_params=params(),
        cost_estimate=pl.CostEstimate(flops=6 * 10**9, bytes_accessed=4 << 20, transcendentals=1 << 22),
        name="attend",
    )(plan, lens, query, k_cache, v_cache, *fresh)


def attend_all_kernel(plan, lens, q_ref, k_ref, v_ref, o_ref, s_ref, vt_ref):
    live = lens[pl.program_id(0)] - plan[0] * k_ref.shape[1]
    attend_request(live, q_ref.at[0], k_ref, v_ref, None, o_ref.at[0], s_ref, vt_ref)


def attend_all(plan, lens, query, k_cache, v_cache):
    requests, span, width = k_cache.shape
    spec = lambda *shape: pl.BlockSpec((1,) + shape, lambda r, plan, lens: (r, 0, 0))
    return pl.pallas_call(
        attend_all_kernel,
        grid_spec=pltpu.PrefetchScalarGridSpec(
            num_scalar_prefetch=2,
            grid=(requests,),
            in_specs=[spec(FEAT, NEW_TOK), spec(span, width), spec(span, width)],
            out_specs=spec(PAY, NEW_TOK),
            scratch_shapes=[pltpu.VMEM((2, span, NEW_TOK), f32), pltpu.VMEM((width, span), bf16)],
        ),
        out_shape=jax.ShapeDtypeStruct((requests, PAY, NEW_TOK), bf16),
        compiler_params=params(),
        name="attend",
    )(plan, lens, query, k_cache, v_cache)


def pool(parts):
    logs = [get_logs(p[FEAT:, :]) for p in parts]
    peak = functools.reduce(jnp.maximum, logs)
    shares = [jnp.exp(x - peak) for x in logs]
    whole = sum(shares)
    shares = [x / whole for x in shares]
    heads = []
    for h in range(HEADS):
        rows = [x[h : h + 1] * p[h * HD : (h + 1) * HD, :].astype(f32) for x, p in zip(shares, parts)]
        heads.append(sum(rows))
    return heads, peak + jnp.log(whole)


def pair_kernel(x_ref, y_ref, o_ref):
    heads, logs = pool([x_ref, y_ref])
    for h, head in enumerate(heads):
        o_ref[h * HD : (h + 1) * HD, :] = head.astype(bf16)
    put_logs(logs, o_ref)


def pair(x, y):
    return pl.pallas_call(
        pair_kernel,
        in_specs=[whole_spec()] * 2,
        out_specs=whole_spec(),
        out_shape=jax.ShapeDtypeStruct(x.shape, x.dtype),
        compiler_params=params(),
        cost_estimate=pl.CostEstimate(flops=10**9, bytes_accessed=1 << 20, transcendentals=0),
        name="pair",
    )(x, y)


def append_kernel(plan, lens, new, k_ref, v_ref, k_out, v_out):
    span = k_ref.shape[1]
    off = lens[plan[pl.program_id(0)]] - plan[pl.num_programs(0)] * span
    window = NEW_TOK + 16
    k_out[...] = k_ref[...]
    v_out[...] = v_ref[...]

    @pl.when((off > -NEW_TOK) & (off < span))
    def _():
        at = pl.multiple_of(jnp.clip(off // 16 * 16, 0, span - window), 16)
        row = lax.broadcasted_iota(jnp.int32, (window, NEW_TOK), 0) + (at - off)
        pick = (row == lax.broadcasted_iota(jnp.int32, (window, NEW_TOK), 1)).astype(bf16)
        width = k_ref.shape[2]
        inside = lax.broadcasted_iota(jnp.int32, (window, width), 0) + (at - off)
        inside = (inside >= 0) & (inside < NEW_TOK)
        both = jnp.dot(pick, new[0], preferred_element_type=f32)
        for old, out, rows in ((k_ref, k_out, both[:, :width]), (v_ref, v_out, both[:, width:])):
            kept = old[0, pl.ds(at, window), :].astype(f32)
            out[0, pl.ds(at, window), :] = jnp.where(inside, rows, kept).astype(bf16)


def append(plan, lens, new, k_cache, v_cache):
    requests, span, width = k_cache.shape
    cache = pl.BlockSpec((1, span, width), lambda i, plan, lens: (plan[i], 0, 0))
    return pl.pallas_call(
        append_kernel,
        grid_spec=pltpu.PrefetchScalarGridSpec(
            num_scalar_prefetch=2,
            grid=(requests,),
            in_specs=[pl.BlockSpec((1, NEW_TOK, 2 * width), lambda i, plan, lens: (i, 0, 0)), cache, cache],
            out_specs=[cache, cache],
        ),
        out_shape=[jax.ShapeDtypeStruct(k_cache.shape, bf16)] * 2,
        compiler_params=params(),
        cost_estimate=pl.CostEstimate(flops=10**9, bytes_accessed=20 << 20, transcendentals=0),
        name="append",
    )(plan, lens, new, k_cache, v_cache)


def merge_kernel(n, t_ref, *refs):
    parts = refs[:n]
    w_ref, send, keep, att = refs[n:]
    step = pl.program_id(0)

    @pl.when(step == 0)
    def _():
        for h, head in enumerate(pool(parts)[0]):
            att[:, h * HD : (h + 1) * HD] = head.T.astype(bf16)

    out = jnp.dot(att[...], w_ref[...], preferred_element_type=f32)

    @pl.when(step < 2)
    def _():
        send[jnp.minimum(step, 1)] = out.astype(bf16)

    @pl.when(step >= 2)
    def _():
        keep[jnp.maximum(step - 2, 0)] = out


SHARE_ORDER = (1, 3, 0, 2)


def share_of(step, t):
    return t ^ jnp.where(step < 2, 2 * step + 1, 2 * step - 4)


def merge(t, parts, w_out):
    n = len(parts)
    rows, features = w_out.shape
    part = features // 4
    shares = pl.BlockSpec((2, NEW_TOK, part), lambda s, t: (0, 0, 0))
    return pl.pallas_call(
        functools.partial(merge_kernel, n),
        grid_spec=pltpu.PrefetchScalarGridSpec(
            num_scalar_prefetch=1,
            grid=(4,),
            in_specs=[pl.BlockSpec((PAY, NEW_TOK), lambda s, t: (0, 0))] * n
            + [pl.BlockSpec((rows, part), lambda s, t: (0, share_of(s, t[0])))],
            out_specs=[shares, shares],
            scratch_shapes=[pltpu.VMEM((NEW_TOK, FEAT), bf16)],
        ),
        out_shape=[
            jax.ShapeDtypeStruct((2, NEW_TOK, part), bf16),
            jax.ShapeDtypeStruct((2, NEW_TOK, part), f32),
        ],
        compiler_params=params(),
        cost_estimate=pl.CostEstimate(flops=2 * 10**9, bytes_accessed=8 << 20, transcendentals=0),
        name="merge",
    )(t, *parts, w_out)


def mlp_kernel(order, t_ref, down_at, x0, x1, x2, x3, gain, wg, wu, *refs):
    downs = refs[:-4]
    send, keep, normed, hidden = refs[-4:]
    step = pl.program_id(0)
    tile = wg.shape[2]
    blocks = len(order) // 4
    depth = wg.shape[1]

    @pl.when(step == 0)
    def _():
        pieces = [x[...].astype(f32) for x in (x0, x1, x2, x3)]
        width = sum(x.shape[1] for x in pieces)
        total = sum(jnp.sum(x * x, axis=-1, keepdims=True) for x in pieces)
        scale = lax.rsqrt(total / width + eps_norm)
        for i, x in enumerate(pieces):
            s = t_ref[0] ^ i
            x = (x * scale * gain[s]).astype(bf16)
            for c in range(blocks):
                normed[s * blocks + c] = x[:, c * depth : (c + 1) * depth]

    @pl.when(step < 4)
    def _():
        gate = up = 0.0
        for i, block in enumerate(order):
            gate += jnp.dot(normed[block], wg[i], preferred_element_type=f32)
            up += jnp.dot(normed[block], wu[i], preferred_element_type=f32)
        hidden[jnp.minimum(step, 3)] = (gate / (1.0 + jnp.exp(-gate)) * up).astype(bf16)

    @pl.when(step >= 4)
    def _():
        columns = []
        for wd in downs:
            out = 0.0
            for i in range(4):
                out += jnp.dot(hidden[i], wd[0, i * tile : (i + 1) * tile, :], preferred_element_type=f32)
            columns.append(out)
        out = jnp.concatenate(columns, axis=1)

        @pl.when(step < 6)
        def _():
            send[jnp.clip(step - 4, 0, 1)] = out.astype(bf16)

        @pl.when(step >= 6)
        def _():
            keep[jnp.clip(step - 6, 0, 1)] = out


def mlp(order, t, down_at, pieces, gain, w_gate, w_up, w_down):
    part = pieces[0].shape[1]
    blocks, depth, units = w_gate.shape
    tile = units // 4
    groups, _, cols = w_down.shape
    each = groups // 4
    piece = pl.BlockSpec((NEW_TOK, part), lambda s, t, at: (0, 0))
    up = pl.BlockSpec((blocks, depth, tile), lambda s, t, at: (0, 0, jnp.minimum(s, 3)))

    def down(c):
        return pl.BlockSpec((1, units, cols), lambda s, t, at: (at[jnp.maximum(s - 4, 0) * each + c], 0, 0))

    shares = pl.BlockSpec((2, NEW_TOK, part), lambda s, t, at: (0, 0, 0))
    return pl.pallas_call(
        functools.partial(mlp_kernel, order),
        grid_spec=pltpu.PrefetchScalarGridSpec(
            num_scalar_prefetch=2,
            grid=(8,),
            in_specs=[piece] * 4
            + [pl.BlockSpec((4, 1, part), lambda s, t, at: (0, 0, 0)), up, up]
            + [down(c) for c in range(each)],
            out_specs=[shares, shares],
            scratch_shapes=[pltpu.VMEM((blocks, NEW_TOK, depth), bf16), pltpu.VMEM((4, NEW_TOK, tile), bf16)],
        ),
        out_shape=[
            jax.ShapeDtypeStruct((2, NEW_TOK, part), bf16),
            jax.ShapeDtypeStruct((2, NEW_TOK, part), f32),
        ],
        compiler_params=params(),
        cost_estimate=pl.CostEstimate(flops=4 * 10**9, bytes_accessed=14 << 20, transcendentals=1 << 18),
        name="mlp",
    )(t, down_at, *pieces, gain.reshape(4, 1, part), w_gate, w_up, *[w_down] * each)


def swap(x, bit, size=4):
    return lax.ppermute(x, "tp", [(i, i ^ bit) for i in range(size)])


def gather_pieces(x):
    across = swap(x, 2)
    beside = swap(x, 1)
    return [x, beside, across, swap(across, 1)]


def scatter_sum(send, keep):
    near = swap(send, 1)
    far = swap((keep[1] + near[1].astype(f32)).astype(bf16), 2)
    return keep[0] + near[0].astype(f32) + far.astype(f32)


def ring_order(groups):
    return list(range(0, groups, 2)) + list(range(groups - 1, 0, -2))


def shards(
    tokens,
    attn_gain,
    w_query,
    w_key,
    w_value,
    w_out,
    mlp_gain,
    w_gate,
    w_up,
    w_down,
    k_cache,
    v_cache,
    prefix_len,
):
    groups = lax.axis_size("grp")
    group = lax.axis_index("grp")
    tp = lax.axis_index("tp")
    t = tp.reshape(1)
    ring = ring_order(groups)
    where = [ring.index(g) for g in range(groups)]
    each = groups // 4

    def gather(x):
        return lax.all_gather(x, "grp", axis=0, axis_index_groups=[ring])

    all_gate, all_up, all_down = gather(w_gate), gather(w_up), gather(w_down)
    shares = [[where[(d ^ i) * each + c] for i in SHARE_ORDER for c in range(each)] for d in range(4)]
    down_at = jnp.array(shares, jnp.int32)[tp]

    own_len = lax.dynamic_index_in_dim(prefix_len, group, keepdims=False)
    half = HD // 2
    inverse = rope_base ** (-2.0 * jnp.arange(half, dtype=f32) / HD)
    positions = own_len + jnp.arange(NEW_TOK, dtype=jnp.int32)
    angles = inverse[:, None] * positions.astype(f32)[None, :]
    query, key_new, value_new = project(
        t, gather_pieces(tokens), attn_gain, w_query, w_key, w_value, jnp.cos(angles), jnp.sin(angles)
    )
    new = gather(jnp.concatenate([key_new, value_new], axis=1))

    if groups == 8:
        pairs = groups // 2
        calls = [
            [r for k in range(pairs) for r in ((g - 2 * k) % groups, ((g - 2 * k) % groups) ^ 1)] + [g]
            for g in range(groups)
        ]
        plan = jnp.array(calls, jnp.int32)[group]

        def turn(x, by):
            return lax.ppermute(x, "grp", [(g, (g + 2 * by) % groups) for g in range(groups)])

        def cross(x):
            return lax.ppermute(x, "grp", [(g, g ^ 1) for g in range(groups)])

        parts = []
        here = query
        for k in range(pairs):
            later = turn(here, 1) if k + 1 < pairs else None
            other = cross(here)
            fresh = () if k else (key_new, value_new)
            if k == 0:
                kept = attend(2 * k, plan, prefix_len, here, k_cache, v_cache, fresh)
            given = cross(attend(2 * k + 1, plan, prefix_len, other, k_cache, v_cache))
            if k:
                kept = attend(2 * k, plan, prefix_len, here, k_cache, v_cache, fresh)
                parts.append(turn(pair(kept, given), -k))
            else:
                parts += [kept, given]
            here = later
    else:
        every = lax.all_gather(query, "grp", axis=0)
        out = attend_all(group.reshape(1), prefix_len, every, k_cache, v_cache)
        back = lax.all_to_all(out, "grp", split_axis=0, concat_axis=0, tiled=True)
        none = jnp.zeros((1,), jnp.int32)
        no_cache = jnp.zeros((1,) + k_cache.shape[1:], bf16)
        own = attend(0, jnp.zeros((2,), jnp.int32), none, query, no_cache, no_cache, (key_new, value_new))
        parts = [back[k] for k in range(groups)] + [own]

    mixed = scatter_sum(*merge(t, parts, w_out))
    first = (tokens.astype(f32) + mixed).astype(bf16)
    down = scatter_sum(*mlp(ring, t, down_at, gather_pieces(first), mlp_gain, all_gate, all_up, all_down))
    result = first.astype(f32) + down
    k_next, v_next = append(jnp.array(ring + [0], jnp.int32).at[groups].set(group), prefix_len, new, k_cache, v_cache)
    return (result, k_next, v_next)


def solution(mesh):
    placed = (
        P("grp", "tp"),
        P(),
        P(None, "tp"),
        P(None, "tp"),
        P(None, "tp"),
        P("tp", None),
        P(),
        P("grp", "tp"),
        P("grp", "tp"),
        P("tp", "grp"),
        P(None, "grp", "tp"),
        P(None, "grp", "tp"),
        P(),
    )
    return jax.shard_map(
        shards,
        mesh=mesh,
        in_specs=placed,
        out_specs=(P("grp", "tp"), P(None, "grp", "tp"), P(None, "grp", "tp")),
        check_vma=False,
    )
```

```python
import functools

import jax
import jax.numpy as jnp
from jax import lax
from jax.experimental import pallas as pl
from jax.experimental.pallas import tpu as pltpu
from jax.sharding import PartitionSpec as P

HD = 64
NEW_TOK = 256
PER_KV = 4
HEADS = 2 * PER_KV
FEAT = HEADS * HD
PAY = FEAT + 4 * HEADS

eps_norm = 1e-05
rope_base = 500000.0
neg_fill = -1e30

f32 = jnp.float32
bf16 = jnp.bfloat16

VMEM_BIG = 63 << 20


def params(limit=VMEM_BIG):
    return pltpu.CompilerParams(vmem_limit_bytes=limit)


def whole_spec():
    return pl.BlockSpec(memory_space=pltpu.VMEM)


def project_kernel(t_ref, x0, x1, x2, x3, gain, wq, wk, wv, cos, sin, q_out, k_out, v_out):
    t = t_ref[0]
    pieces = [x[...].astype(f32) for x in (x0, x1, x2, x3)]
    width = sum(x.shape[1] for x in pieces)
    total = sum(jnp.sum(x * x, axis=-1, keepdims=True) for x in pieces)
    scale = lax.rsqrt(total / width + eps_norm)
    q = k = v = 0.0
    for i, x in enumerate(pieces):
        s = t ^ i
        n = (x * scale * gain[s]).astype(bf16)
        q += jnp.dot(n, wq[s], preferred_element_type=f32)
        k += jnp.dot(n, wk[s], preferred_element_type=f32)
        v += jnp.dot(n, wv[s], preferred_element_type=f32)
    c, s = cos[...], sin[...]

    def rotate(cols):
        a, b = cols[: HD // 2], cols[HD // 2 :]
        return [a * c - b * s, b * c + a * s]

    qt = q.T
    rows = []
    for h in range(qt.shape[0] // HD):
        rows += rotate(qt[h * HD : (h + 1) * HD])
    q_out[...] = (jnp.concatenate(rows, axis=0).astype(bf16) * 0.125).astype(bf16)
    kt = k.T
    rows = []
    for h in range(kt.shape[0] // HD):
        rows += rotate(kt[h * HD : (h + 1) * HD])
    k_out[...] = jnp.concatenate(rows, axis=0).T.astype(bf16)
    v_out[...] = v.astype(bf16)


def project(t, pieces, gain, w_query, w_key, w_value, cos, sin):
    tp = len(pieces)
    part = pieces[0].shape[1]
    smem = pl.BlockSpec(memory_space=pltpu.SMEM)
    return pl.pallas_call(
        project_kernel,
        in_specs=[smem] + [whole_spec()] * 10,
        out_specs=[whole_spec()] * 3,
        out_shape=[
            jax.ShapeDtypeStruct((w_query.shape[1], NEW_TOK), bf16),
            jax.ShapeDtypeStruct((NEW_TOK, w_key.shape[1]), bf16),
            jax.ShapeDtypeStruct((NEW_TOK, w_value.shape[1]), bf16),
        ],
        compiler_params=params(),
        cost_estimate=pl.CostEstimate(flops=2 * 10**9, bytes_accessed=4 << 20, transcendentals=0),
        name="project",
    )(
        t,
        *pieces,
        gain.reshape(tp, 1, part),
        w_query.reshape(tp, part, -1),
        w_key.reshape(tp, part, -1),
        w_value.reshape(tp, part, -1),
        cos,
        sin,
    )


def put_logs(logs, o_ref):
    high = logs.astype(bf16).astype(f32)
    rest = logs - high
    middle = rest.astype(bf16).astype(f32)
    low = rest - middle
    rows = jnp.concatenate([high, middle, low, jnp.zeros_like(low)], axis=0)
    o_ref[FEAT:, :] = rows.astype(bf16)


def get_logs(rows):
    rows = rows.astype(f32)
    return rows[:HEADS] + rows[HEADS : 2 * HEADS] + rows[2 * HEADS : 3 * HEADS]


def attend_request(live, q_ref, k_ref, v_ref, fresh, o_ref, s_ref, vt_ref):
    span = k_ref.shape[1]
    chunk = min(512, span)
    zero = jnp.zeros((HD, NEW_TOK), bf16)

    def run(cached, masked):
        pieces = [(c * chunk, chunk) for c in range(span // chunk)] if cached else []
        if cached:
            vt_ref[:, :span] = v_ref[0].T
        if fresh:
            pieces.append((span, NEW_TOK))
            vt_ref[:, span:] = fresh[1][...].T

        def scores(h):
            own = q_ref[h * HD : (h + 1) * HD, :]
            wide = jnp.concatenate([own, zero] if h < PER_KV else [zero, own], axis=0)
            top = None
            for lo, rows in pieces:
                keys = k_ref[0, lo : lo + rows, :] if lo < span else fresh[0][...]
                s = jnp.dot(keys, wide, preferred_element_type=f32)
                at = lax.broadcasted_iota(jnp.int32, s.shape, 0)
                if lo >= span:
                    s = jnp.where(at <= lax.broadcasted_iota(jnp.int32, s.shape, 1), s, neg_fill)
                elif masked:
                    s = jnp.where(at < live - lo, s, neg_fill)
                s_ref[h % 2, lo : lo + rows, :] = s
                here = jnp.max(s, axis=0, keepdims=True)
                top = here if top is None else jnp.maximum(top, here)
            return top

        top = scores(0)
        logs = []
        for h in range(HEADS):
            later = scores(h + 1) if h + 1 < HEADS else None
            j = h // PER_KV
            acc = jnp.zeros((HD + 16, NEW_TOK), f32)
            for lo, rows in pieces:
                p = jnp.exp(s_ref[h % 2, lo : lo + rows, :] - top).astype(bf16)
                values = jnp.concatenate(
                    [vt_ref[j * HD : (j + 1) * HD, lo : lo + rows], jnp.ones((16, rows), bf16)], axis=0
                )
                acc = acc + jnp.dot(values, p, preferred_element_type=f32)
            total = acc[HD : HD + 1]
            o_ref[h * HD : (h + 1) * HD, :] = (acc[:HD] / total).astype(bf16)
            logs.append(top + jnp.log(total))
            top = later
        put_logs(jnp.concatenate(logs, axis=0), o_ref)

    pl.when(live >= span)(lambda: run(True, False))
    pl.when((live > 0) & (live < span))(lambda: run(True, True))

    @pl.when(live <= 0)
    def _():
        if fresh:
            run(False, False)
        else:
            o_ref[:FEAT, :] = jnp.zeros((FEAT, NEW_TOK), bf16)
            put_logs(jnp.full((HEADS, NEW_TOK), neg_fill, f32), o_ref)


def attend_kernel(call, fresh, chained, plan, lens, q_ref, k_ref, v_ref, *refs):
    fresh, refs = (refs[:2], refs[2:]) if fresh else (None, refs)
    o_ref, k_out, v_out, s_ref, vt_ref, sems = refs[2 if chained else 0 :]
    copies = [
        pltpu.make_async_copy(k_ref, k_out.at[pl.ds(plan[call], 1)], sems.at[0]),
        pltpu.make_async_copy(v_ref, v_out.at[pl.ds(plan[call], 1)], sems.at[1]),
    ]
    for copy in copies:
        copy.start()
    live = lens[plan[call]] - plan[plan.shape[0] - 1] * k_ref.shape[1]
    attend_request(live, q_ref, k_ref, v_ref, fresh, o_ref, s_ref, vt_ref)
    for copy in copies:
        copy.wait()


def attend(call, plan, lens, query, k_cache, v_cache, fresh=(), copied=()):
    span, width = k_cache.shape[1:]
    cache = pl.BlockSpec((1, span, width), lambda i, plan, lens: (plan[call], 0, 0))
    flat = lambda shape: pl.BlockSpec(shape, lambda i, plan, lens: (0, 0))
    anywhere = pl.BlockSpec(memory_space=pl.ANY)
    long = span + (NEW_TOK if fresh else 0)
    before = 2 + 3 + len(fresh)
    return pl.pallas_call(
        functools.partial(attend_kernel, call, bool(fresh), bool(copied)),
        grid_spec=pltpu.PrefetchScalarGridSpec(
            num_scalar_prefetch=2,
            grid=(1,),
            in_specs=[flat(query.shape), cache, cache]
            + [flat(x.shape) for x in fresh]
            + [anywhere] * len(copied),
            out_specs=[flat((PAY, NEW_TOK)), anywhere, anywhere],
            scratch_shapes=[
                pltpu.VMEM((2, long, NEW_TOK), f32),
                pltpu.VMEM((width, long), bf16),
                pltpu.SemaphoreType.DMA((2,)),
            ],
        ),
        out_shape=[
            jax.ShapeDtypeStruct((PAY, NEW_TOK), bf16),
            jax.ShapeDtypeStruct(k_cache.shape, bf16),
            jax.ShapeDtypeStruct(v_cache.shape, bf16),
        ],
        input_output_aliases={before: 1, before + 1: 2} if copied else {},
        compiler_params=params(),
        cost_estimate=pl.CostEstimate(flops=6 * 10**9, bytes_accessed=4 << 20, transcendentals=1 << 22),
        name="attend",
    )(plan, lens, query, k_cache, v_cache, *fresh, *copied)


def attend_all_kernel(plan, lens, q_ref, k_ref, v_ref, o_ref, s_ref, vt_ref):
    live = lens[pl.program_id(0)] - plan[0] * k_ref.shape[1]
    attend_request(live, q_ref.at[0], k_ref, v_ref, None, o_ref.at[0], s_ref, vt_ref)


def attend_all(plan, lens, query, k_cache, v_cache):
    requests, span, width = k_cache.shape
    spec = lambda *shape: pl.BlockSpec((1,) + shape, lambda r, plan, lens: (r, 0, 0))
    return pl.pallas_call(
        attend_all_kernel,
        grid_spec=pltpu.PrefetchScalarGridSpec(
            num_scalar_prefetch=2,
            grid=(requests,),
            in_specs=[spec(FEAT, NEW_TOK), spec(span, width), spec(span, width)],
            out_specs=spec(PAY, NEW_TOK),
            scratch_shapes=[pltpu.VMEM((2, span, NEW_TOK), f32), pltpu.VMEM((width, span), bf16)],
        ),
        out_shape=jax.ShapeDtypeStruct((requests, PAY, NEW_TOK), bf16),
        compiler_params=params(),
        name="attend",
    )(plan, lens, query, k_cache, v_cache)


def pool(parts):
    logs = [get_logs(p[FEAT:, :]) for p in parts]
    peak = functools.reduce(jnp.maximum, logs)
    shares = [jnp.exp(x - peak) for x in logs]
    whole = sum(shares)
    shares = [x / whole for x in shares]
    heads = []
    for h in range(HEADS):
        rows = [x[h : h + 1] * p[h * HD : (h + 1) * HD, :].astype(f32) for x, p in zip(shares, parts)]
        heads.append(sum(rows))
    return heads, peak + jnp.log(whole)


def pair_kernel(x_ref, y_ref, o_ref):
    heads, logs = pool([x_ref, y_ref])
    for h, head in enumerate(heads):
        o_ref[h * HD : (h + 1) * HD, :] = head.astype(bf16)
    put_logs(logs, o_ref)


def pair(x, y):
    return pl.pallas_call(
        pair_kernel,
        in_specs=[whole_spec()] * 2,
        out_specs=whole_spec(),
        out_shape=jax.ShapeDtypeStruct(x.shape, x.dtype),
        compiler_params=params(),
        cost_estimate=pl.CostEstimate(flops=10**9, bytes_accessed=1 << 20, transcendentals=0),
        name="pair",
    )(x, y)


def append_kernel(count, plan, lens, *refs):
    news = refs[:count]
    k_out, v_out, k_buf, v_buf, sems = refs[count + 2 :]
    _, span, width = k_out.shape
    requests, window, _ = k_buf.shape
    rows_of = [news[c].at[i] for c in range(count) for i in range(news[c].shape[0])]

    def each_touched(act):
        for i in range(requests):
            r = plan[i]
            off = lens[r] - plan[plan.shape[0] - 1] * span

            @pl.when((off > -NEW_TOK) & (off < span))
            def _():
                at = pl.multiple_of(jnp.clip(off // 16 * 16, 0, span - window), 16)
                far = [k_out.at[r, pl.ds(at, window)], v_out.at[r, pl.ds(at, window)]]
                near = [k_buf.at[i], v_buf.at[i]]

                def copies(out):
                    pairs = [(near[c], far[c]) if out else (far[c], near[c]) for c in range(2)]
                    return [pltpu.make_async_copy(*pair, sems.at[i, c]) for c, pair in enumerate(pairs)]

                act(i, at - off, near, copies)

    def load(i, shift, near, copies):
        for copy in copies(False):
            copy.start()

    def change(i, shift, near, copies):
        row = lax.broadcasted_iota(jnp.int32, (window, NEW_TOK), 0) + shift
        pick = (row == lax.broadcasted_iota(jnp.int32, (window, NEW_TOK), 1)).astype(bf16)
        inside = lax.broadcasted_iota(jnp.int32, (window, width), 0) + shift
        inside = (inside >= 0) & (inside < NEW_TOK)
        both = jnp.dot(pick, rows_of[i][...], preferred_element_type=f32)
        for copy in copies(False):
            copy.wait()
        for ref, rows in zip(near, (both[:, :width], both[:, width:])):
            ref[...] = jnp.where(inside, rows, ref[...].astype(f32)).astype(bf16)
        for copy in copies(True):
            copy.start()

    def finish(i, shift, near, copies):
        for copy in copies(True):
            copy.wait()

    each_touched(load)
    each_touched(change)
    each_touched(finish)


def append(plan, lens, news, k_next, v_next):
    requests, _, width = k_next.shape
    window = NEW_TOK + 16
    anywhere = pl.BlockSpec(memory_space=pl.ANY)
    count = len(news)
    return pl.pallas_call(
        functools.partial(append_kernel, count),
        grid_spec=pltpu.PrefetchScalarGridSpec(
            num_scalar_prefetch=2,
            grid=(1,),
            in_specs=[pl.BlockSpec(x.shape, lambda i, plan, lens: (0, 0, 0)) for x in news] + [anywhere] * 2,
            out_specs=[anywhere] * 2,
            scratch_shapes=[pltpu.VMEM((requests, window, width), bf16)] * 2
            + [pltpu.SemaphoreType.DMA((requests, 2))],
        ),
        out_shape=[jax.ShapeDtypeStruct(k_next.shape, bf16)] * 2,
        input_output_aliases={2 + count: 0, 3 + count: 1},
        compiler_params=params(),
        cost_estimate=pl.CostEstimate(flops=10**9, bytes_accessed=4 << 20, transcendentals=0),
        name="append",
    )(plan, lens, *news, k_next, v_next)


def merge_kernel(n, t_ref, *refs):
    parts = refs[:n]
    w_ref, send, keep, att = refs[n:]
    step = pl.program_id(0)

    @pl.when(step == 0)
    def _():
        for h, head in enumerate(pool(parts)[0]):
            att[:, h * HD : (h + 1) * HD] = head.T.astype(bf16)

    out = jnp.dot(att[...], w_ref[...], preferred_element_type=f32)

    @pl.when(step < 2)
    def _():
        send[jnp.minimum(step, 1)] = out.astype(bf16)

    @pl.when(step >= 2)
    def _():
        keep[jnp.maximum(step - 2, 0)] = out


SHARE_ORDER = (1, 3, 0, 2)


def share_of(step, t):
    return t ^ jnp.where(step < 2, 2 * step + 1, 2 * step - 4)


def merge(t, parts, w_out):
    n = len(parts)
    rows, features = w_out.shape
    part = features // 4
    shares = pl.BlockSpec((2, NEW_TOK, part), lambda s, t: (0, 0, 0))
    return pl.pallas_call(
        functools.partial(merge_kernel, n),
        grid_spec=pltpu.PrefetchScalarGridSpec(
            num_scalar_prefetch=1,
            grid=(4,),
            in_specs=[pl.BlockSpec((PAY, NEW_TOK), lambda s, t: (0, 0))] * n
            + [pl.BlockSpec((rows, part), lambda s, t: (0, share_of(s, t[0])))],
            out_specs=[shares, shares],
            scratch_shapes=[pltpu.VMEM((NEW_TOK, FEAT), bf16)],
        ),
        out_shape=[
            jax.ShapeDtypeStruct((2, NEW_TOK, part), bf16),
            jax.ShapeDtypeStruct((2, NEW_TOK, part), f32),
        ],
        compiler_params=params(),
        cost_estimate=pl.CostEstimate(flops=2 * 10**9, bytes_accessed=8 << 20, transcendentals=0),
        name="merge",
    )(t, *parts, w_out)


def expand_kernel(order, t_ref, both, beyond, gain, wg, wu, hidden, normed):
    blocks = len(order) // 4
    depth = wg.shape[1]

    @pl.when(pl.program_id(0) == 0)
    def _():
        pieces = [x[i].astype(f32) for i in range(2) for x in (both, beyond)]
        width = sum(x.shape[1] for x in pieces)
        total = sum(jnp.sum(x * x, axis=-1, keepdims=True) for x in pieces)
        scale = lax.rsqrt(total / width + eps_norm)
        for i, x in enumerate(pieces):
            s = t_ref[0] ^ i
            x = (x * scale * gain[s]).astype(bf16)
            for c in range(blocks):
                normed[s * blocks + c] = x[:, c * depth : (c + 1) * depth]

    gate = up = 0.0
    for i, block in enumerate(order):
        gate += jnp.dot(normed[block], wg[i], preferred_element_type=f32)
        up += jnp.dot(normed[block], wu[i], preferred_element_type=f32)
    hidden[0] = (gate / (1.0 + jnp.exp(-gate)) * up).astype(bf16)


def expand(order, t, both, beyond, gain, w_gate_up):
    part = both.shape[2]
    blocks, depth, units = w_gate_up.shape
    tile = units // 8
    piece = pl.BlockSpec(both.shape, lambda s, t: (0, 0, 0))
    return pl.pallas_call(
        functools.partial(expand_kernel, order),
        grid_spec=pltpu.PrefetchScalarGridSpec(
            num_scalar_prefetch=1,
            grid=(4,),
            in_specs=[piece] * 2
            + [
                pl.BlockSpec((4, 1, part), lambda s, t: (0, 0, 0)),
                pl.BlockSpec((blocks, depth, tile), lambda s, t: (0, 0, s)),
                pl.BlockSpec((blocks, depth, tile), lambda s, t: (0, 0, 4 + s)),
            ],
            out_specs=pl.BlockSpec((1, NEW_TOK, tile), lambda s, t: (s, 0, 0)),
            scratch_shapes=[pltpu.VMEM((blocks, NEW_TOK, depth), bf16)],
        ),
        out_shape=jax.ShapeDtypeStruct((4, NEW_TOK, tile), bf16),
        compiler_params=params(),
        cost_estimate=pl.CostEstimate(flops=3 * 10**9, bytes_accessed=9 << 20, transcendentals=1 << 18),
        name="expand",
    )(t, both, beyond, gain.reshape(4, 1, part), w_gate_up, w_gate_up)


def reduce_kernel(t_ref, down_at, hidden, *refs):
    downs = refs[:-2]
    send, keep = refs[-2:]
    step = pl.program_id(0)
    tile = hidden.shape[2]
    columns = []
    for wd in downs:
        out = 0.0
        for i in range(4):
            out += jnp.dot(hidden[i], wd[0, i * tile : (i + 1) * tile, :], preferred_element_type=f32)
        columns.append(out)
    out = jnp.concatenate(columns, axis=1)

    @pl.when(step < 2)
    def _():
        send[jnp.minimum(step, 1)] = out.astype(bf16)

    @pl.when(step >= 2)
    def _():
        keep[jnp.maximum(step - 2, 0)] = out


def reduce(t, down_at, hidden, w_down):
    groups, units, cols = w_down.shape
    each = groups // 4
    part = each * cols

    def down(c):
        return pl.BlockSpec((1, units, cols), lambda s, t, at: (at[s * each + c], 0, 0))

    shares = pl.BlockSpec((2, NEW_TOK, part), lambda s, t, at: (0, 0, 0))
    return pl.pallas_call(
        reduce_kernel,
        grid_spec=pltpu.PrefetchScalarGridSpec(
            num_scalar_prefetch=2,
            grid=(4,),
            in_specs=[pl.BlockSpec(hidden.shape, lambda s, t, at: (0, 0, 0))] + [down(c) for c in range(each)],
            out_specs=[shares, shares],
        ),
        out_shape=[
            jax.ShapeDtypeStruct((2, NEW_TOK, part), bf16),
            jax.ShapeDtypeStruct((2, NEW_TOK, part), f32),
        ],
        compiler_params=params(),
        cost_estimate=pl.CostEstimate(flops=10**9, bytes_accessed=5 << 20, transcendentals=0),
        name="reduce",
    )(t, down_at, hidden, *[w_down] * each)


def swap(x, bit, size=4):
    return lax.ppermute(x, "tp", [(i, i ^ bit) for i in range(size)])


def gather_pieces(x):
    across = swap(x, 2)
    beside = swap(x, 1)
    return [x, beside, across, swap(across, 1)]


def scatter_sum(send, keep):
    near = swap(send, 1)
    far = swap((keep[1] + near[1].astype(f32)).astype(bf16), 2)
    return keep[0] + near[0].astype(f32) + far.astype(f32)


def ring_order(groups):
    return list(range(0, groups, 2)) + list(range(groups - 1, 0, -2))


def shards(
    tokens,
    attn_gain,
    w_query,
    w_key,
    w_value,
    w_out,
    mlp_gain,
    w_gate,
    w_up,
    w_down,
    k_cache,
    v_cache,
    prefix_len,
):
    groups = lax.axis_size("grp")
    group = lax.axis_index("grp")
    tp = lax.axis_index("tp")
    t = tp.reshape(1)
    ring = ring_order(groups)
    where = [ring.index(g) for g in range(groups)]
    each = groups // 4

    def gather(x):
        return lax.all_gather(x, "grp", axis=0, axis_index_groups=[ring])

    all_gate_up = gather(jnp.concatenate([w_gate, w_up], axis=1))
    all_down = gather(w_down)
    shares = [[where[(d ^ i) * each + c] for i in SHARE_ORDER for c in range(each)] for d in range(4)]
    down_at = jnp.array(shares, jnp.int32)[tp]

    own_len = lax.dynamic_index_in_dim(prefix_len, group, keepdims=False)
    half = HD // 2
    inverse = rope_base ** (-2.0 * jnp.arange(half, dtype=f32) / HD)
    positions = own_len + jnp.arange(NEW_TOK, dtype=jnp.int32)
    angles = inverse[:, None] * positions.astype(f32)[None, :]
    token_pieces = gather_pieces(tokens)
    query, key_new, value_new = project(
        t, token_pieces, attn_gain, w_query, w_key, w_value, jnp.cos(angles), jnp.sin(angles)
    )
    new = jnp.concatenate([key_new, value_new], axis=1)

    def turn(x, by):
        return lax.ppermute(x, "grp", [(g, (g + 2 * by) % groups) for g in range(groups)])

    def cross(x):
        return lax.ppermute(x, "grp", [(g, g ^ 1) for g in range(groups)])

    if groups == 8:
        pairs = groups // 2
        calls = [
            [r for k in range(pairs) for r in ((g - 2 * k) % groups, ((g - 2 * k) % groups) ^ 1)] + [g]
            for g in range(groups)
        ]
        plan = jnp.array(calls, jnp.int32)[group]

        own = [query]
        for k in range(1, pairs):
            own.append(turn(own[-1], 1))
        other = [cross(x) for x in own]
        copied = ()

        def call(k, crossed):
            nonlocal copied
            fresh = () if k or crossed else (key_new, value_new)
            source = other[k] if crossed else own[k]
            out, *copied = attend(2 * k + crossed, plan, prefix_len, source, k_cache, v_cache, fresh, copied)
            return out

        def merged(k, kept, given, following):
            both, following[0][following[1]] = lax.optimization_barrier((pair(kept, given), following[0][following[1]]))
            return turn(both, -k)

        parts = [call(0, 0)]
        kept = call(1, 0)
        given = cross(call(1, 1))
        for k in range(2, pairs):
            later = cross(call(k, 1))
            parts.append(merged(k - 1, kept, given, (own, k)))
            kept, given = call(k, 0), later
        parts.append(merged(pairs - 1, kept, given, (other, 0)))
        parts.append(cross(call(0, 1)))
    else:
        every = lax.all_gather(query, "grp", axis=0)
        out = attend_all(group.reshape(1), prefix_len, every, k_cache, v_cache)
        back = lax.all_to_all(out, "grp", split_axis=0, concat_axis=0, tiled=True)
        none = jnp.zeros((1,), jnp.int32)
        no_cache = jnp.zeros((1,) + k_cache.shape[1:], bf16)
        own, *_ = attend(0, jnp.zeros((2,), jnp.int32), none, query, no_cache, no_cache, (key_new, value_new))
        parts = [back[k] for k in range(groups)] + [own]
        news = [gather(new)]
        new_plan = jnp.array(ring + [0], jnp.int32).at[groups].set(group)
        copied = (k_cache, v_cache)

    send, keep = merge(t, parts, w_out)
    half = (keep + swap(send, 1).astype(f32)).astype(bf16)
    mixed = half.astype(f32) + swap(half[::-1], 2).astype(f32)
    both = (jnp.stack([token_pieces[0], token_pieces[2]]).astype(f32) + mixed).astype(bf16)
    beyond = swap(both, 1)
    first = both[0]
    hidden = expand(ring, t, both, beyond, mlp_gain, all_gate_up)
    send, keep = reduce(t, down_at, hidden, all_down)
    if groups == 8:
        both, new = lax.optimization_barrier((both, new))
        news = [new] + [turn(new, k) for k in range(1, pairs)]
        send, *news[1::2] = lax.optimization_barrier((send, *news[1::2]))
        early = jnp.stack([news[0], news[1], news[3]])
        news = [early, cross(early), news[2][None], cross(news[2])[None]]
        slots = [0, 2, 6, 1, 3, 7, 4, 5]
        new_plan = jnp.array([[call[s] for s in slots] + [call[-1]] for call in calls], jnp.int32)[group]
    down = scatter_sum(send, keep)
    result = first.astype(f32) + down
    k_next, v_next = append(new_plan, prefix_len, news, *copied)
    return (result, k_next, v_next)


def solution(mesh):
    placed = (
        P("grp", "tp"),
        P(),
        P(None, "tp"),
        P(None, "tp"),
        P(None, "tp"),
        P("tp", None),
        P(),
        P("grp", "tp"),
        P("grp", "tp"),
        P("tp", "grp"),
        P(None, "grp", "tp"),
        P(None, "grp", "tp"),
        P(),
    )
    return jax.shard_map(
        shards,
        mesh=mesh,
        in_specs=placed,
        out_specs=(P("grp", "tp"), P(None, "grp", "tp"), P(None, "grp", "tp")),
        check_vma=False,
    )
```

```python
import functools

import jax
import jax.numpy as jnp
from jax import lax
from jax.experimental import pallas as pl
from jax.experimental.pallas import tpu as pltpu
from jax.sharding import PartitionSpec as P

HD = 64
NEW_TOK = 256
PER_KV = 4
HEADS = 2 * PER_KV
FEAT = HEADS * HD
PAY = FEAT + 4 * HEADS

eps_norm = 1e-05
rope_base = 500000.0
neg_fill = -1e30

f32 = jnp.float32
bf16 = jnp.bfloat16

VMEM_BIG = 63 << 20


def params(limit=VMEM_BIG):
    return pltpu.CompilerParams(vmem_limit_bytes=limit)


def whole_spec():
    return pl.BlockSpec(memory_space=pltpu.VMEM)


def project_kernel(t_ref, x0, x1, x2, x3, gain, wq, wk, wv, cos, sin, q_out, k_out, v_out):
    t = t_ref[0]
    pieces = [x[...].astype(f32) for x in (x0, x1, x2, x3)]
    width = sum(x.shape[1] for x in pieces)
    total = sum(jnp.sum(x * x, axis=-1, keepdims=True) for x in pieces)
    scale = lax.rsqrt(total / width + eps_norm)
    q = k = v = 0.0
    for i, x in enumerate(pieces):
        s = t ^ i
        n = (x * scale * gain[s]).astype(bf16)
        q += jnp.dot(n, wq[s], preferred_element_type=f32)
        k += jnp.dot(n, wk[s], preferred_element_type=f32)
        v += jnp.dot(n, wv[s], preferred_element_type=f32)
    c, s = cos[...], sin[...]

    def rotate(cols):
        a, b = cols[: HD // 2], cols[HD // 2 :]
        return [a * c - b * s, b * c + a * s]

    qt = q.T
    rows = []
    for h in range(qt.shape[0] // HD):
        rows += rotate(qt[h * HD : (h + 1) * HD])
    q_out[...] = (jnp.concatenate(rows, axis=0).astype(bf16) * 0.125).astype(bf16)
    kt = k.T
    rows = []
    for h in range(kt.shape[0] // HD):
        rows += rotate(kt[h * HD : (h + 1) * HD])
    k_out[...] = jnp.concatenate(rows, axis=0).T.astype(bf16)
    v_out[...] = v.astype(bf16)


def project(t, pieces, gain, w_query, w_key, w_value, cos, sin):
    tp = len(pieces)
    part = pieces[0].shape[1]
    smem = pl.BlockSpec(memory_space=pltpu.SMEM)
    return pl.pallas_call(
        project_kernel,
        in_specs=[smem] + [whole_spec()] * 10,
        out_specs=[whole_spec()] * 3,
        out_shape=[
            jax.ShapeDtypeStruct((w_query.shape[1], NEW_TOK), bf16),
            jax.ShapeDtypeStruct((NEW_TOK, w_key.shape[1]), bf16),
            jax.ShapeDtypeStruct((NEW_TOK, w_value.shape[1]), bf16),
        ],
        compiler_params=params(),
        cost_estimate=pl.CostEstimate(flops=2 * 10**9, bytes_accessed=4 << 20, transcendentals=0),
        name="project",
    )(
        t,
        *pieces,
        gain.reshape(tp, 1, part),
        w_query.reshape(tp, part, -1),
        w_key.reshape(tp, part, -1),
        w_value.reshape(tp, part, -1),
        cos,
        sin,
    )


def put_logs(logs, o_ref):
    high = logs.astype(bf16).astype(f32)
    rest = logs - high
    middle = rest.astype(bf16).astype(f32)
    low = rest - middle
    rows = jnp.concatenate([high, middle, low, jnp.zeros_like(low)], axis=0)
    o_ref[FEAT:, :] = rows.astype(bf16)


def get_logs(rows):
    rows = rows.astype(f32)
    return rows[:HEADS] + rows[HEADS : 2 * HEADS] + rows[2 * HEADS : 3 * HEADS]


def attend_request(live, q_ref, k_ref, v_ref, fresh, o_ref, s_ref, vt_ref):
    span = k_ref.shape[1]
    chunk = min(512, span)
    zero = jnp.zeros((HD, NEW_TOK), bf16)

    def run(cached, masked):
        pieces = [(c * chunk, chunk) for c in range(span // chunk)] if cached else []
        if cached:
            vt_ref[:, :span] = v_ref[0].T
        if fresh:
            pieces.append((span, NEW_TOK))
            vt_ref[:, span:] = fresh[1][...].T

        def scores(h):
            own = q_ref[h * HD : (h + 1) * HD, :]
            wide = jnp.concatenate([own, zero] if h < PER_KV else [zero, own], axis=0)
            top = None
            for lo, rows in pieces:
                keys = k_ref[0, lo : lo + rows, :] if lo < span else fresh[0][...]
                s = jnp.dot(keys, wide, preferred_element_type=f32)
                at = lax.broadcasted_iota(jnp.int32, s.shape, 0)
                if lo >= span:
                    s = jnp.where(at <= lax.broadcasted_iota(jnp.int32, s.shape, 1), s, neg_fill)
                elif masked:
                    s = jnp.where(at < live - lo, s, neg_fill)
                s_ref[h % 2, lo : lo + rows, :] = s
                here = jnp.max(s, axis=0, keepdims=True)
                top = here if top is None else jnp.maximum(top, here)
            return top

        top = scores(0)
        logs = []
        for h in range(HEADS):
            later = scores(h + 1) if h + 1 < HEADS else None
            j = h // PER_KV
            acc = jnp.zeros((HD + 16, NEW_TOK), f32)
            for lo, rows in pieces:
                p = jnp.exp(s_ref[h % 2, lo : lo + rows, :] - top).astype(bf16)
                values = jnp.concatenate(
                    [vt_ref[j * HD : (j + 1) * HD, lo : lo + rows], jnp.ones((16, rows), bf16)], axis=0
                )
                acc = acc + jnp.dot(values, p, preferred_element_type=f32)
            total = acc[HD : HD + 1]
            o_ref[h * HD : (h + 1) * HD, :] = (acc[:HD] / total).astype(bf16)
            logs.append(top + jnp.log(total))
            top = later
        put_logs(jnp.concatenate(logs, axis=0), o_ref)

    pl.when(live >= span)(lambda: run(True, False))
    pl.when((live > 0) & (live < span))(lambda: run(True, True))

    @pl.when(live <= 0)
    def _():
        if fresh:
            run(False, False)
        else:
            o_ref[:FEAT, :] = jnp.zeros((FEAT, NEW_TOK), bf16)
            put_logs(jnp.full((HEADS, NEW_TOK), neg_fill, f32), o_ref)


def attend_kernel(call, fresh, chained, plan, lens, q_ref, k_ref, v_ref, *refs):
    fresh, refs = (refs[:2], refs[2:]) if fresh else (None, refs)
    o_ref, k_out, v_out, s_ref, vt_ref, sems = refs[2 if chained else 0 :]
    copies = [
        pltpu.make_async_copy(k_ref, k_out.at[pl.ds(plan[call], 1)], sems.at[0]),
        pltpu.make_async_copy(v_ref, v_out.at[pl.ds(plan[call], 1)], sems.at[1]),
    ]
    for copy in copies:
        copy.start()
    live = lens[plan[call]] - plan[plan.shape[0] - 1] * k_ref.shape[1]
    attend_request(live, q_ref, k_ref, v_ref, fresh, o_ref, s_ref, vt_ref)
    for copy in copies:
        copy.wait()


def attend(call, plan, lens, query, k_cache, v_cache, fresh=(), copied=()):
    span, width = k_cache.shape[1:]
    cache = pl.BlockSpec((1, span, width), lambda i, plan, lens: (plan[call], 0, 0))
    flat = lambda shape: pl.BlockSpec(shape, lambda i, plan, lens: (0, 0))
    anywhere = pl.BlockSpec(memory_space=pl.ANY)
    long = span + (NEW_TOK if fresh else 0)
    before = 2 + 3 + len(fresh)
    return pl.pallas_call(
        functools.partial(attend_kernel, call, bool(fresh), bool(copied)),
        grid_spec=pltpu.PrefetchScalarGridSpec(
            num_scalar_prefetch=2,
            grid=(1,),
            in_specs=[flat(query.shape), cache, cache]
            + [flat(x.shape) for x in fresh]
            + [anywhere] * len(copied),
            out_specs=[flat((PAY, NEW_TOK)), anywhere, anywhere],
            scratch_shapes=[
                pltpu.VMEM((2, long, NEW_TOK), f32),
                pltpu.VMEM((width, long), bf16),
                pltpu.SemaphoreType.DMA((2,)),
            ],
        ),
        out_shape=[
            jax.ShapeDtypeStruct((PAY, NEW_TOK), bf16),
            jax.ShapeDtypeStruct(k_cache.shape, bf16),
            jax.ShapeDtypeStruct(v_cache.shape, bf16),
        ],
        input_output_aliases={before: 1, before + 1: 2} if copied else {},
        compiler_params=params(),
        cost_estimate=pl.CostEstimate(flops=6 * 10**9, bytes_accessed=4 << 20, transcendentals=1 << 22),
        name="attend",
    )(plan, lens, query, k_cache, v_cache, *fresh, *copied)


def attend_all_kernel(plan, lens, q_ref, k_ref, v_ref, o_ref, s_ref, vt_ref):
    live = lens[pl.program_id(0)] - plan[0] * k_ref.shape[1]
    attend_request(live, q_ref.at[0], k_ref, v_ref, None, o_ref.at[0], s_ref, vt_ref)


def attend_all(plan, lens, query, k_cache, v_cache):
    requests, span, width = k_cache.shape
    spec = lambda *shape: pl.BlockSpec((1,) + shape, lambda r, plan, lens: (r, 0, 0))
    return pl.pallas_call(
        attend_all_kernel,
        grid_spec=pltpu.PrefetchScalarGridSpec(
            num_scalar_prefetch=2,
            grid=(requests,),
            in_specs=[spec(FEAT, NEW_TOK), spec(span, width), spec(span, width)],
            out_specs=spec(PAY, NEW_TOK),
            scratch_shapes=[pltpu.VMEM((2, span, NEW_TOK), f32), pltpu.VMEM((width, span), bf16)],
        ),
        out_shape=jax.ShapeDtypeStruct((requests, PAY, NEW_TOK), bf16),
        compiler_params=params(),
        name="attend",
    )(plan, lens, query, k_cache, v_cache)


def pool(parts):
    logs = [get_logs(p[FEAT:, :]) for p in parts]
    peak = functools.reduce(jnp.maximum, logs)
    shares = [jnp.exp(x - peak) for x in logs]
    whole = sum(shares)
    shares = [x / whole for x in shares]
    heads = []
    for h in range(HEADS):
        rows = [x[h : h + 1] * p[h * HD : (h + 1) * HD, :].astype(f32) for x, p in zip(shares, parts)]
        heads.append(sum(rows))
    return heads, peak + jnp.log(whole)


def pair_kernel(x_ref, y_ref, o_ref):
    heads, logs = pool([x_ref, y_ref])
    for h, head in enumerate(heads):
        o_ref[h * HD : (h + 1) * HD, :] = head.astype(bf16)
    put_logs(logs, o_ref)


def pair(x, y):
    return pl.pallas_call(
        pair_kernel,
        in_specs=[whole_spec()] * 2,
        out_specs=whole_spec(),
        out_shape=jax.ShapeDtypeStruct(x.shape, x.dtype),
        compiler_params=params(),
        cost_estimate=pl.CostEstimate(flops=10**9, bytes_accessed=1 << 20, transcendentals=0),
        name="pair",
    )(x, y)


def append_kernel(count, plan, lens, *refs):
    news = refs[:count]
    k_out, v_out, k_buf, v_buf, sems = refs[count + 2 :]
    _, span, width = k_out.shape
    requests, window, _ = k_buf.shape
    rows_of = [news[c].at[i] for c in range(count) for i in range(news[c].shape[0])]

    def each_touched(act):
        for i in range(requests):
            r = plan[i]
            off = lens[r] - plan[plan.shape[0] - 1] * span

            @pl.when((off > -NEW_TOK) & (off < span))
            def _():
                at = pl.multiple_of(jnp.clip(off // 16 * 16, 0, span - window), 16)
                far = [k_out.at[r, pl.ds(at, window)], v_out.at[r, pl.ds(at, window)]]
                near = [k_buf.at[i], v_buf.at[i]]

                def copies(out):
                    pairs = [(near[c], far[c]) if out else (far[c], near[c]) for c in range(2)]
                    return [pltpu.make_async_copy(*pair, sems.at[i, c]) for c, pair in enumerate(pairs)]

                act(i, at - off, near, copies)

    def load(i, shift, near, copies):
        for copy in copies(False):
            copy.start()

    def change(i, shift, near, copies):
        row = lax.broadcasted_iota(jnp.int32, (window, NEW_TOK), 0) + shift
        pick = (row == lax.broadcasted_iota(jnp.int32, (window, NEW_TOK), 1)).astype(bf16)
        inside = lax.broadcasted_iota(jnp.int32, (window, width), 0) + shift
        inside = (inside >= 0) & (inside < NEW_TOK)
        both = jnp.dot(pick, rows_of[i][...], preferred_element_type=f32)
        for copy in copies(False):
            copy.wait()
        for ref, rows in zip(near, (both[:, :width], both[:, width:])):
            ref[...] = jnp.where(inside, rows, ref[...].astype(f32)).astype(bf16)
        for copy in copies(True):
            copy.start()

    def finish(i, shift, near, copies):
        for copy in copies(True):
            copy.wait()

    each_touched(load)
    each_touched(change)
    each_touched(finish)


def append(plan, lens, news, k_next, v_next):
    requests, _, width = k_next.shape
    window = NEW_TOK + 16
    anywhere = pl.BlockSpec(memory_space=pl.ANY)
    count = len(news)
    return pl.pallas_call(
        functools.partial(append_kernel, count),
        grid_spec=pltpu.PrefetchScalarGridSpec(
            num_scalar_prefetch=2,
            grid=(1,),
            in_specs=[pl.BlockSpec(x.shape, lambda i, plan, lens: (0, 0, 0)) for x in news] + [anywhere] * 2,
            out_specs=[anywhere] * 2,
            scratch_shapes=[pltpu.VMEM((requests, window, width), bf16)] * 2
            + [pltpu.SemaphoreType.DMA((requests, 2))],
        ),
        out_shape=[jax.ShapeDtypeStruct(k_next.shape, bf16)] * 2,
        input_output_aliases={2 + count: 0, 3 + count: 1},
        compiler_params=params(),
        cost_estimate=pl.CostEstimate(flops=10**9, bytes_accessed=4 << 20, transcendentals=0),
        name="append",
    )(plan, lens, *news, k_next, v_next)


def merge_kernel(n, t_ref, *refs):
    parts = refs[:n]
    w_ref, send, keep, att = refs[n:]
    step = pl.program_id(0)

    @pl.when(step == 0)
    def _():
        for h, head in enumerate(pool(parts)[0]):
            att[:, h * HD : (h + 1) * HD] = head.T.astype(bf16)

    out = jnp.dot(att[...], w_ref[...], preferred_element_type=f32)

    @pl.when(step < 2)
    def _():
        send[jnp.minimum(step, 1)] = out.astype(bf16)

    @pl.when(step >= 2)
    def _():
        keep[jnp.maximum(step - 2, 0)] = out


SHARE_ORDER = (1, 3, 0, 2)


def share_of(step, t):
    return t ^ jnp.where(step < 2, 2 * step + 1, 2 * step - 4)


def merge(t, parts, w_out):
    n = len(parts)
    rows, features = w_out.shape
    part = features // 4
    shares = pl.BlockSpec((2, NEW_TOK, part), lambda s, t: (0, 0, 0))
    return pl.pallas_call(
        functools.partial(merge_kernel, n),
        grid_spec=pltpu.PrefetchScalarGridSpec(
            num_scalar_prefetch=1,
            grid=(4,),
            in_specs=[pl.BlockSpec((PAY, NEW_TOK), lambda s, t: (0, 0))] * n
            + [pl.BlockSpec((rows, part), lambda s, t: (0, share_of(s, t[0])))],
            out_specs=[shares, shares],
            scratch_shapes=[pltpu.VMEM((NEW_TOK, FEAT), bf16)],
        ),
        out_shape=[
            jax.ShapeDtypeStruct((2, NEW_TOK, part), bf16),
            jax.ShapeDtypeStruct((2, NEW_TOK, part), f32),
        ],
        compiler_params=params(),
        cost_estimate=pl.CostEstimate(flops=2 * 10**9, bytes_accessed=8 << 20, transcendentals=0),
        name="merge",
    )(t, *parts, w_out)


def pack_kernel(gate, up, down, out):
    units, width = down.shape
    at = 0
    for w in (gate, up):
        for i in range(0, units, width):
            out[at : at + width, :] = w[:, i : i + width]
            at += width
    out[at:, :] = down[...]


def pack(w_gate, w_up, w_down):
    units, width = w_down.shape
    return pl.pallas_call(
        pack_kernel,
        in_specs=[whole_spec()] * 3,
        out_specs=whole_spec(),
        out_shape=jax.ShapeDtypeStruct((3 * units, width), bf16),
        compiler_params=params(),
        cost_estimate=pl.CostEstimate(flops=0, bytes_accessed=3 << 20, transcendentals=0),
        name="pack",
    )(w_gate, w_up, w_down)


def mlp_kernel(one, t_ref, at_ref, down_at, both, beyond, gain, *refs):
    weights, (send, keep, normed, hidden, wg, wu, wd, sems) = refs[:-8], refs[-8:]
    w_gate, w_up, w_down = weights * 3 if one else weights
    tiles, blocks, depth, tile = wg.shape
    places, units, cols = wd.shape
    each = places // 4

    def load_up(side, s):
        first = side * tiles * depth if one else 0
        rows = pl.ds(first + s * depth, depth) if one else slice(None)
        columns = slice(None) if one else pl.ds(s * tile, tile)
        source, target = ((w_gate, wg), (w_up, wu))[side]
        return pltpu.make_async_copy(source.at[:, rows, columns], target.at[s], sems.at[2 * s + side])

    def load_down(i):
        rows = pl.ds(2 * units if one else 0, units)
        return pltpu.make_async_copy(w_down.at[down_at[i], rows], wd.at[i], sems.at[2 * tiles + i])

    for s in range(tiles):
        load_up(0, s).start()
        load_up(1, s).start()
    for i in range(places):
        load_down(i).start()

    pieces = [x[i].astype(f32) for i in range(2) for x in (both, beyond)]
    width = sum(x.shape[1] for x in pieces)
    total = sum(jnp.sum(x * x, axis=-1, keepdims=True) for x in pieces)
    scale = lax.rsqrt(total / width + eps_norm)
    for i, x in enumerate(pieces):
        s = t_ref[0] ^ i
        x = (x * scale * gain[s]).astype(bf16)
        count = x.shape[1] // depth
        for c in range(count):
            at = pl.multiple_of(at_ref[s * count + c] * depth, depth)
            normed[:, pl.ds(at, depth)] = x[:, c * depth : (c + 1) * depth]

    for s in range(tiles):
        load_up(0, s).wait()
        load_up(1, s).wait()
        gate = jnp.dot(normed[...], wg[s].reshape(blocks * depth, tile), preferred_element_type=f32)
        up = jnp.dot(normed[...], wu[s].reshape(blocks * depth, tile), preferred_element_type=f32)
        hidden[:, s * tile : (s + 1) * tile] = (gate / (1.0 + jnp.exp(-gate)) * up).astype(bf16)

    for i in range(places):
        load_down(i).wait()
        out = jnp.dot(hidden[...], wd[i], preferred_element_type=f32)
        place = (i // each % 2, slice(None), slice(i % each * cols, (i % each + 1) * cols))
        if i < places // 2:
            send[place] = out.astype(bf16)
        else:
            keep[place] = out


def mlp(t, at, down_at, both, beyond, gain, weights):
    part = both.shape[2]
    one = len(weights) == 1
    groups, units, cols = weights[-1].shape
    blocks, depth, _ = weights[0].shape
    if one:
        units, depth = units // 3, cols
    tile = units // 4
    smem = pl.BlockSpec(memory_space=pltpu.SMEM)
    up = pltpu.VMEM((4, blocks, depth, tile), bf16)
    return pl.pallas_call(
        functools.partial(mlp_kernel, one),
        in_specs=[smem] * 3 + [whole_spec()] * 3 + [pl.BlockSpec(memory_space=pl.ANY)] * len(weights),
        out_specs=[whole_spec()] * 2,
        out_shape=[
            jax.ShapeDtypeStruct((2, NEW_TOK, part), bf16),
            jax.ShapeDtypeStruct((2, NEW_TOK, part), f32),
        ],
        scratch_shapes=[
            pltpu.VMEM((NEW_TOK, 4 * part), bf16),
            pltpu.VMEM((NEW_TOK, units), bf16),
            up,
            up,
            pltpu.VMEM((groups, units, cols), bf16),
            pltpu.SemaphoreType.DMA((8 + groups,)),
        ],
        compiler_params=params(),
        cost_estimate=pl.CostEstimate(flops=8 * 10**9, bytes_accessed=28 << 20, transcendentals=1 << 18),
        name="mlp",
    )(t, at, down_at, both, beyond, gain.reshape(4, 1, part), *weights)


def swap(x, bit, size=4):
    return lax.ppermute(x, "tp", [(i, i ^ bit) for i in range(size)])


def gather_pieces(x):
    across = swap(x, 2)
    beside = swap(x, 1)
    return [x, beside, across, swap(across, 1)]


def ring_order(groups):
    return list(range(0, groups, 2)) + list(range(groups - 1, 0, -2))


def shards(
    tokens,
    attn_gain,
    w_query,
    w_key,
    w_value,
    w_out,
    mlp_gain,
    w_gate,
    w_up,
    w_down,
    k_cache,
    v_cache,
    prefix_len,
):
    groups = lax.axis_size("grp")
    group = lax.axis_index("grp")
    tp = lax.axis_index("tp")
    t = tp.reshape(1)
    ring = ring_order(groups)
    where = [ring.index(g) for g in range(groups)]
    each = groups // 4

    def gather(x):
        return lax.all_gather(x, "grp", axis=0, axis_index_groups=[ring])

    if w_gate.shape[1] == 4 * w_down.shape[1]:
        weights = [gather(pack(w_gate, w_up, w_down))]
        feature_at = jnp.array(where, jnp.int32)
    else:
        weights = [lax.all_gather(w, "grp", axis=0, tiled=True).reshape(4, -1, w.shape[1]) for w in (w_gate, w_up)]
        weights.append(gather(w_down))
        feature_at = jnp.arange(4, dtype=jnp.int32)
    shares = [[where[(d ^ i) * each + c] for i in SHARE_ORDER for c in range(each)] for d in range(4)]
    down_at = jnp.array(shares, jnp.int32)[tp]

    own_len = lax.dynamic_index_in_dim(prefix_len, group, keepdims=False)
    half = HD // 2
    inverse = rope_base ** (-2.0 * jnp.arange(half, dtype=f32) / HD)
    positions = own_len + jnp.arange(NEW_TOK, dtype=jnp.int32)
    angles = inverse[:, None] * positions.astype(f32)[None, :]
    token_pieces = gather_pieces(tokens)
    query, key_new, value_new = project(
        t, token_pieces, attn_gain, w_query, w_key, w_value, jnp.cos(angles), jnp.sin(angles)
    )
    new = jnp.concatenate([key_new, value_new], axis=1)

    def turn(x, by):
        return lax.ppermute(x, "grp", [(g, (g + 2 * by) % groups) for g in range(groups)])

    def cross(x):
        return lax.ppermute(x, "grp", [(g, g ^ 1) for g in range(groups)])

    if groups == 8:
        pairs = groups // 2
        calls = [
            [r for k in range(pairs) for r in ((g - 2 * k) % groups, ((g - 2 * k) % groups) ^ 1)] + [g]
            for g in range(groups)
        ]
        plan = jnp.array(calls, jnp.int32)[group]

        own = [query]
        for k in range(1, pairs):
            own.append(turn(own[-1], 1))
        other = [cross(x) for x in own]
        copied = ()

        def call(k, crossed):
            nonlocal copied
            fresh = () if k or crossed else (key_new, value_new)
            source = other[k] if crossed else own[k]
            out, *copied = attend(2 * k + crossed, plan, prefix_len, source, k_cache, v_cache, fresh, copied)
            return out

        def merged(k, kept, given, following):
            both, following[0][following[1]] = lax.optimization_barrier((pair(kept, given), following[0][following[1]]))
            return turn(both, -k)

        parts = [call(0, 0)]
        kept = call(1, 0)
        given = cross(call(1, 1))
        for k in range(2, pairs):
            later = cross(call(k, 1))
            parts.append(merged(k - 1, kept, given, (own, k)))
            kept, given = call(k, 0), later
        parts.append(merged(pairs - 1, kept, given, (other, 0)))
        parts.append(cross(call(0, 1)))
    else:
        every = lax.all_gather(query, "grp", axis=0)
        out = attend_all(group.reshape(1), prefix_len, every, k_cache, v_cache)
        back = lax.all_to_all(out, "grp", split_axis=0, concat_axis=0, tiled=True)
        none = jnp.zeros((1,), jnp.int32)
        no_cache = jnp.zeros((1,) + k_cache.shape[1:], bf16)
        own, *_ = attend(0, jnp.zeros((2,), jnp.int32), none, query, no_cache, no_cache, (key_new, value_new))
        parts = [back[k] for k in range(groups)] + [own]
        news = [gather(new)]
        plan = jnp.array(ring + [0], jnp.int32).at[groups].set(group)
        copied = (k_cache, v_cache)

    send, keep = merge(t, parts, w_out)
    half = (keep + swap(send, 1).astype(f32)).astype(bf16)
    mixed = half.astype(f32) + swap(half[::-1], 2).astype(f32)
    both = (jnp.stack([token_pieces[0], token_pieces[2]]).astype(f32) + mixed).astype(bf16)
    beyond = swap(both, 1)
    first = both[0]
    if groups == 8:
        both, new = lax.optimization_barrier((both, new))
        news = [turn(new, k) for k in range(1, pairs)]
    send, keep = mlp(t, feature_at, down_at, both, beyond, mlp_gain, weights)
    if groups == 8:
        send, keep, *news = lax.optimization_barrier((send, keep, *news))
        news = jnp.stack([new, *news])
        news = [news, cross(news)]
        slots = [0, 2, 4, 6, 1, 3, 5, 7]
        plan = jnp.array([[call[s] for s in slots] + [call[-1]] for call in calls], jnp.int32)[group]
    near = swap(send, 1)
    far = (keep[1] + near[1].astype(f32)).astype(bf16)
    down = keep[0] + near[0].astype(f32) + swap(far, 2).astype(f32)
    result = first.astype(f32) + down
    result, plan = lax.optimization_barrier((result, plan))
    k_next, v_next = append(plan, prefix_len, news, *copied)
    return (result, k_next, v_next)


def solution(mesh):
    placed = (
        P("grp", "tp"),
        P(),
        P(None, "tp"),
        P(None, "tp"),
        P(None, "tp"),
        P("tp", None),
        P(),
        P("grp", "tp"),
        P("grp", "tp"),
        P("tp", "grp"),
        P(None, "grp", "tp"),
        P(None, "grp", "tp"),
        P(),
    )
    return jax.shard_map(
        shards,
        mesh=mesh,
        in_specs=placed,
        out_specs=(P("grp", "tp"), P(None, "grp", "tp"), P(None, "grp", "tp")),
        check_vma=False,
    )
```

```python
import functools

import jax
import jax.numpy as jnp
from jax import lax
from jax.experimental import pallas as pl
from jax.experimental.pallas import tpu as pltpu
from jax.sharding import PartitionSpec as P

HD = 64
NEW_TOK = 256
PER_KV = 4
HEADS = 2 * PER_KV
FEAT = HEADS * HD
PAY = FEAT + 4 * HEADS

eps_norm = 1e-05
rope_base = 500000.0
neg_fill = -1e30

f32 = jnp.float32
bf16 = jnp.bfloat16

VMEM_BIG = 63 << 20


def params(limit=VMEM_BIG):
    return pltpu.CompilerParams(vmem_limit_bytes=limit)


def whole_spec():
    return pl.BlockSpec(memory_space=pltpu.VMEM)


def project_kernel(t_ref, x0, x1, x2, x3, gain, wq, wk, wv, cos, sin, q_out, k_out, v_out):
    t = t_ref[0]
    pieces = [x[...].astype(f32) for x in (x0, x1, x2, x3)]
    width = sum(x.shape[1] for x in pieces)
    total = sum(jnp.sum(x * x, axis=-1, keepdims=True) for x in pieces)
    scale = lax.rsqrt(total / width + eps_norm)
    q = k = v = 0.0
    for i, x in enumerate(pieces):
        s = t ^ i
        n = (x * scale * gain[s]).astype(bf16)
        q += jnp.dot(n, wq[s], preferred_element_type=f32)
        k += jnp.dot(n, wk[s], preferred_element_type=f32)
        v += jnp.dot(n, wv[s], preferred_element_type=f32)
    c, s = cos[...], sin[...]

    def rotate(cols):
        a, b = cols[: HD // 2], cols[HD // 2 :]
        return [a * c - b * s, b * c + a * s]

    qt = q.T
    rows = []
    for h in range(qt.shape[0] // HD):
        rows += rotate(qt[h * HD : (h + 1) * HD])
    q_out[...] = (jnp.concatenate(rows, axis=0).astype(bf16) * 0.125).astype(bf16)
    kt = k.T
    rows = []
    for h in range(kt.shape[0] // HD):
        rows += rotate(kt[h * HD : (h + 1) * HD])
    k_out[...] = jnp.concatenate(rows, axis=0).T.astype(bf16)
    v_out[...] = v.astype(bf16)


def project(t, pieces, gain, w_query, w_key, w_value, cos, sin):
    tp = len(pieces)
    part = pieces[0].shape[1]
    smem = pl.BlockSpec(memory_space=pltpu.SMEM)
    return pl.pallas_call(
        project_kernel,
        in_specs=[smem] + [whole_spec()] * 10,
        out_specs=[whole_spec()] * 3,
        out_shape=[
            jax.ShapeDtypeStruct((w_query.shape[1], NEW_TOK), bf16),
            jax.ShapeDtypeStruct((NEW_TOK, w_key.shape[1]), bf16),
            jax.ShapeDtypeStruct((NEW_TOK, w_value.shape[1]), bf16),
        ],
        compiler_params=params(),
        cost_estimate=pl.CostEstimate(flops=2 * 10**9, bytes_accessed=4 << 20, transcendentals=0),
        name="project",
    )(
        t,
        *pieces,
        gain.reshape(tp, 1, part),
        w_query.reshape(tp, part, -1),
        w_key.reshape(tp, part, -1),
        w_value.reshape(tp, part, -1),
        cos,
        sin,
    )


def put_logs(logs, o_ref):
    high = logs.astype(bf16).astype(f32)
    rest = logs - high
    middle = rest.astype(bf16).astype(f32)
    low = rest - middle
    rows = jnp.concatenate([high, middle, low, jnp.zeros_like(low)], axis=0)
    o_ref[FEAT:, :] = rows.astype(bf16)


def get_logs(rows):
    rows = rows.astype(f32)
    return rows[:HEADS] + rows[HEADS : 2 * HEADS] + rows[2 * HEADS : 3 * HEADS]


def attend_request(live, q_ref, k_ref, v_ref, fresh, o_ref, s_ref, vt_ref):
    span = k_ref.shape[1]
    chunk = min(512, span)
    zero = jnp.zeros((HD, NEW_TOK), bf16)

    def run(cached, masked):
        pieces = [(c * chunk, chunk) for c in range(span // chunk)] if cached else []
        if cached:
            vt_ref[:, :span] = v_ref[0].T
        if fresh:
            pieces.append((span, NEW_TOK))
            vt_ref[:, span:] = fresh[1][...].T

        def scores(h):
            own = q_ref[h * HD : (h + 1) * HD, :]
            wide = jnp.concatenate([own, zero] if h < PER_KV else [zero, own], axis=0)
            top = None
            for lo, rows in pieces:
                keys = k_ref[0, lo : lo + rows, :] if lo < span else fresh[0][...]
                s = jnp.dot(keys, wide, preferred_element_type=f32)
                at = lax.broadcasted_iota(jnp.int32, s.shape, 0)
                if lo >= span:
                    s = jnp.where(at <= lax.broadcasted_iota(jnp.int32, s.shape, 1), s, neg_fill)
                elif masked:
                    s = jnp.where(at < live - lo, s, neg_fill)
                s_ref[h % 2, lo : lo + rows, :] = s
                here = jnp.max(s, axis=0, keepdims=True)
                top = here if top is None else jnp.maximum(top, here)
            return top

        top = scores(0)
        logs = []
        for h in range(HEADS):
            later = scores(h + 1) if h + 1 < HEADS else None
            j = h // PER_KV
            acc = jnp.zeros((HD + 16, NEW_TOK), f32)
            for lo, rows in pieces:
                p = jnp.exp(s_ref[h % 2, lo : lo + rows, :] - top).astype(bf16)
                values = jnp.concatenate(
                    [vt_ref[j * HD : (j + 1) * HD, lo : lo + rows], jnp.ones((16, rows), bf16)], axis=0
                )
                acc = acc + jnp.dot(values, p, preferred_element_type=f32)
            total = acc[HD : HD + 1]
            o_ref[h * HD : (h + 1) * HD, :] = (acc[:HD] / total).astype(bf16)
            logs.append(top + jnp.log(total))
            top = later
        put_logs(jnp.concatenate(logs, axis=0), o_ref)

    pl.when(live >= span)(lambda: run(True, False))
    pl.when((live > 0) & (live < span))(lambda: run(True, True))

    @pl.when(live <= 0)
    def _():
        if fresh:
            run(False, False)
        else:
            o_ref[:FEAT, :] = jnp.zeros((FEAT, NEW_TOK), bf16)
            put_logs(jnp.full((HEADS, NEW_TOK), neg_fill, f32), o_ref)


def attend_kernel(call, fresh, chained, plan, lens, q_ref, k_ref, v_ref, *refs):
    fresh, refs = (refs[:2], refs[2:]) if fresh else (None, refs)
    o_ref, k_out, v_out, s_ref, vt_ref, sems = refs[2 if chained else 0 :]
    copies = [
        pltpu.make_async_copy(k_ref, k_out.at[pl.ds(plan[call], 1)], sems.at[0]),
        pltpu.make_async_copy(v_ref, v_out.at[pl.ds(plan[call], 1)], sems.at[1]),
    ]
    for copy in copies:
        copy.start()
    live = lens[plan[call]] - plan[plan.shape[0] - 1] * k_ref.shape[1]
    attend_request(live, q_ref, k_ref, v_ref, fresh, o_ref, s_ref, vt_ref)
    for copy in copies:
        copy.wait()


def attend(call, plan, lens, query, k_cache, v_cache, fresh=(), copied=()):
    span, width = k_cache.shape[1:]
    cache = pl.BlockSpec((1, span, width), lambda i, plan, lens: (plan[call], 0, 0))
    flat = lambda shape: pl.BlockSpec(shape, lambda i, plan, lens: (0, 0))
    anywhere = pl.BlockSpec(memory_space=pl.ANY)
    long = span + (NEW_TOK if fresh else 0)
    before = 2 + 3 + len(fresh)
    return pl.pallas_call(
        functools.partial(attend_kernel, call, bool(fresh), bool(copied)),
        grid_spec=pltpu.PrefetchScalarGridSpec(
            num_scalar_prefetch=2,
            grid=(1,),
            in_specs=[flat(query.shape), cache, cache]
            + [flat(x.shape) for x in fresh]
            + [anywhere] * len(copied),
            out_specs=[flat((PAY, NEW_TOK)), anywhere, anywhere],
            scratch_shapes=[
                pltpu.VMEM((2, long, NEW_TOK), f32),
                pltpu.VMEM((width, long), bf16),
                pltpu.SemaphoreType.DMA((2,)),
            ],
        ),
        out_shape=[
            jax.ShapeDtypeStruct((PAY, NEW_TOK), bf16),
            jax.ShapeDtypeStruct(k_cache.shape, bf16),
            jax.ShapeDtypeStruct(v_cache.shape, bf16),
        ],
        input_output_aliases={before: 1, before + 1: 2} if copied else {},
        compiler_params=params(),
        cost_estimate=pl.CostEstimate(flops=6 * 10**9, bytes_accessed=4 << 20, transcendentals=1 << 22),
        name="attend",
    )(plan, lens, query, k_cache, v_cache, *fresh, *copied)


def attend_all_kernel(plan, lens, q_ref, k_ref, v_ref, o_ref, s_ref, vt_ref):
    live = lens[pl.program_id(0)] - plan[0] * k_ref.shape[1]
    attend_request(live, q_ref.at[0], k_ref, v_ref, None, o_ref.at[0], s_ref, vt_ref)


def attend_all(plan, lens, query, k_cache, v_cache):
    requests, span, width = k_cache.shape
    spec = lambda *shape: pl.BlockSpec((1,) + shape, lambda r, plan, lens: (r, 0, 0))
    return pl.pallas_call(
        attend_all_kernel,
        grid_spec=pltpu.PrefetchScalarGridSpec(
            num_scalar_prefetch=2,
            grid=(requests,),
            in_specs=[spec(FEAT, NEW_TOK), spec(span, width), spec(span, width)],
            out_specs=spec(PAY, NEW_TOK),
            scratch_shapes=[pltpu.VMEM((2, span, NEW_TOK), f32), pltpu.VMEM((width, span), bf16)],
        ),
        out_shape=jax.ShapeDtypeStruct((requests, PAY, NEW_TOK), bf16),
        compiler_params=params(),
        name="attend",
    )(plan, lens, query, k_cache, v_cache)


def pool(parts):
    logs = [get_logs(p[FEAT:, :]) for p in parts]
    peak = functools.reduce(jnp.maximum, logs)
    shares = [jnp.exp(x - peak) for x in logs]
    whole = sum(shares)
    shares = [x / whole for x in shares]
    heads = []
    for h in range(HEADS):
        rows = [x[h : h + 1] * p[h * HD : (h + 1) * HD, :].astype(f32) for x, p in zip(shares, parts)]
        heads.append(sum(rows))
    return heads, peak + jnp.log(whole)


def pair_kernel(x_ref, y_ref, o_ref):
    heads, logs = pool([x_ref, y_ref])
    for h, head in enumerate(heads):
        o_ref[h * HD : (h + 1) * HD, :] = head.astype(bf16)
    put_logs(logs, o_ref)


def pair(x, y):
    return pl.pallas_call(
        pair_kernel,
        in_specs=[whole_spec()] * 2,
        out_specs=whole_spec(),
        out_shape=jax.ShapeDtypeStruct(x.shape, x.dtype),
        compiler_params=params(),
        cost_estimate=pl.CostEstimate(flops=10**9, bytes_accessed=1 << 20, transcendentals=0),
        name="pair",
    )(x, y)


def append_kernel(count, plan, lens, *refs):
    news = refs[:count]
    k_out, v_out, k_buf, v_buf, sems = refs[count + 2 :]
    _, span, width = k_out.shape
    requests, window, _ = k_buf.shape
    rows_of = [news[c].at[i] for c in range(count) for i in range(news[c].shape[0])]

    def each_touched(act):
        for i in range(requests):
            r = plan[i]
            off = lens[r] - plan[plan.shape[0] - 1] * span

            @pl.when((off > -NEW_TOK) & (off < span))
            def _():
                at = pl.multiple_of(jnp.clip(off // 16 * 16, 0, span - window), 16)
                far = [k_out.at[r, pl.ds(at, window)], v_out.at[r, pl.ds(at, window)]]
                near = [k_buf.at[i], v_buf.at[i]]

                def copies(out):
                    pairs = [(near[c], far[c]) if out else (far[c], near[c]) for c in range(2)]
                    return [pltpu.make_async_copy(*pair, sems.at[i, c]) for c, pair in enumerate(pairs)]

                act(i, at - off, near, copies)

    def load(i, shift, near, copies):
        for copy in copies(False):
            copy.start()

    def change(i, shift, near, copies):
        row = lax.broadcasted_iota(jnp.int32, (window, NEW_TOK), 0) + shift
        pick = (row == lax.broadcasted_iota(jnp.int32, (window, NEW_TOK), 1)).astype(bf16)
        inside = lax.broadcasted_iota(jnp.int32, (window, width), 0) + shift
        inside = (inside >= 0) & (inside < NEW_TOK)
        both = jnp.dot(pick, rows_of[i][...], preferred_element_type=f32)
        for copy in copies(False):
            copy.wait()
        for ref, rows in zip(near, (both[:, :width], both[:, width:])):
            ref[...] = jnp.where(inside, rows, ref[...].astype(f32)).astype(bf16)
        for copy in copies(True):
            copy.start()

    def finish(i, shift, near, copies):
        for copy in copies(True):
            copy.wait()

    each_touched(load)
    each_touched(change)
    each_touched(finish)


def append(plan, lens, news, k_next, v_next):
    requests, _, width = k_next.shape
    window = NEW_TOK + 16
    anywhere = pl.BlockSpec(memory_space=pl.ANY)
    count = len(news)
    return pl.pallas_call(
        functools.partial(append_kernel, count),
        grid_spec=pltpu.PrefetchScalarGridSpec(
            num_scalar_prefetch=2,
            grid=(1,),
            in_specs=[pl.BlockSpec(x.shape, lambda i, plan, lens: (0, 0, 0)) for x in news] + [anywhere] * 2,
            out_specs=[anywhere] * 2,
            scratch_shapes=[pltpu.VMEM((requests, window, width), bf16)] * 2
            + [pltpu.SemaphoreType.DMA((requests, 2))],
        ),
        out_shape=[jax.ShapeDtypeStruct(k_next.shape, bf16)] * 2,
        input_output_aliases={2 + count: 0, 3 + count: 1},
        compiler_params=params(),
        cost_estimate=pl.CostEstimate(flops=10**9, bytes_accessed=4 << 20, transcendentals=0),
        name="append",
    )(plan, lens, *news, k_next, v_next)


def merge_kernel(n, t_ref, *refs):
    parts = refs[:n]
    w_ref, send, keep, att = refs[n:]
    step = pl.program_id(0)

    @pl.when(step == 0)
    def _():
        for h, head in enumerate(pool(parts)[0]):
            att[:, h * HD : (h + 1) * HD] = head.T.astype(bf16)

    out = jnp.dot(att[...], w_ref[...], preferred_element_type=f32)

    @pl.when(step < 2)
    def _():
        send[jnp.minimum(step, 1)] = out.astype(bf16)

    @pl.when(step >= 2)
    def _():
        keep[jnp.maximum(step - 2, 0)] = out


SHARE_ORDER = (1, 3, 0, 2)


def share_of(step, t):
    return t ^ jnp.where(step < 2, 2 * step + 1, 2 * step - 4)


def merge(t, parts, w_out):
    n = len(parts)
    rows, features = w_out.shape
    part = features // 4
    shares = pl.BlockSpec((2, NEW_TOK, part), lambda s, t: (0, 0, 0))
    return pl.pallas_call(
        functools.partial(merge_kernel, n),
        grid_spec=pltpu.PrefetchScalarGridSpec(
            num_scalar_prefetch=1,
            grid=(4,),
            in_specs=[pl.BlockSpec((PAY, NEW_TOK), lambda s, t: (0, 0))] * n
            + [pl.BlockSpec((rows, part), lambda s, t: (0, share_of(s, t[0])))],
            out_specs=[shares, shares],
            scratch_shapes=[pltpu.VMEM((NEW_TOK, FEAT), bf16)],
        ),
        out_shape=[
            jax.ShapeDtypeStruct((2, NEW_TOK, part), bf16),
            jax.ShapeDtypeStruct((2, NEW_TOK, part), f32),
        ],
        compiler_params=params(),
        cost_estimate=pl.CostEstimate(flops=2 * 10**9, bytes_accessed=8 << 20, transcendentals=0),
        name="merge",
    )(t, *parts, w_out)


def pack_kernel(gate, up, down, out):
    units, width = down.shape
    at = 0
    for w in (gate, up):
        for i in range(0, units, width):
            out[at : at + width, :] = w[:, i : i + width]
            at += width
    out[at:, :] = down[...]


def pack(w_gate, w_up, w_down):
    units, width = w_down.shape
    return pl.pallas_call(
        pack_kernel,
        in_specs=[whole_spec()] * 3,
        out_specs=whole_spec(),
        out_shape=jax.ShapeDtypeStruct((3 * units, width), bf16),
        compiler_params=params(),
        cost_estimate=pl.CostEstimate(flops=0, bytes_accessed=3 << 20, transcendentals=0),
        name="pack",
    )(w_gate, w_up, w_down)


def mlp_kernel(one, t_ref, at_ref, down_at, both, beyond, gain, *refs):
    weights, (send, keep, normed, hidden, wg, wu, wd, sems) = refs[:-8], refs[-8:]
    w_gate, w_up, w_down = weights * 3 if one else weights
    tiles, blocks, depth, tile = wg.shape
    places, units, cols = wd.shape
    each = places // 4

    def load_up(side, s):
        first = side * tiles * depth if one else 0
        rows = pl.ds(first + s * depth, depth) if one else slice(None)
        columns = slice(None) if one else pl.ds(s * tile, tile)
        source, target = ((w_gate, wg), (w_up, wu))[side]
        return pltpu.make_async_copy(source.at[:, rows, columns], target.at[s], sems.at[2 * s + side])

    def load_down(i):
        rows = pl.ds(2 * units if one else 0, units)
        return pltpu.make_async_copy(w_down.at[down_at[i], rows], wd.at[i], sems.at[2 * tiles + i])

    for s in range(tiles):
        load_up(0, s).start()
        load_up(1, s).start()
    for i in range(places):
        load_down(i).start()

    pieces = [x[i].astype(f32) for i in range(2) for x in (both, beyond)]
    width = sum(x.shape[1] for x in pieces)
    total = sum(jnp.sum(x * x, axis=-1, keepdims=True) for x in pieces)
    scale = lax.rsqrt(total / width + eps_norm)
    for i, x in enumerate(pieces):
        s = t_ref[0] ^ i
        x = (x * scale * gain[s]).astype(bf16)
        count = x.shape[1] // depth
        for c in range(count):
            at = pl.multiple_of(at_ref[s * count + c] * depth, depth)
            normed[:, pl.ds(at, depth)] = x[:, c * depth : (c + 1) * depth]

    for s in range(tiles):
        load_up(0, s).wait()
        load_up(1, s).wait()
        gate = jnp.dot(normed[...], wg[s].reshape(blocks * depth, tile), preferred_element_type=f32)
        up = jnp.dot(normed[...], wu[s].reshape(blocks * depth, tile), preferred_element_type=f32)
        hidden[:, s * tile : (s + 1) * tile] = (gate / (1.0 + jnp.exp(-gate)) * up).astype(bf16)

    for i in range(places):
        load_down(i).wait()
        out = jnp.dot(hidden[...], wd[i], preferred_element_type=f32)
        place = (i // each % 2, slice(None), slice(i % each * cols, (i % each + 1) * cols))
        if i < places // 2:
            send[place] = out.astype(bf16)
        else:
            keep[place] = out


def mlp(t, at, down_at, both, beyond, gain, weights):
    part = both.shape[2]
    one = len(weights) == 1
    groups, units, cols = weights[-1].shape
    blocks, depth, _ = weights[0].shape
    if one:
        units, depth = units // 3, cols
    tile = units // 4
    smem = pl.BlockSpec(memory_space=pltpu.SMEM)
    up = pltpu.VMEM((4, blocks, depth, tile), bf16)
    return pl.pallas_call(
        functools.partial(mlp_kernel, one),
        in_specs=[smem] * 3 + [whole_spec()] * 3 + [pl.BlockSpec(memory_space=pl.ANY)] * len(weights),
        out_specs=[whole_spec()] * 2,
        out_shape=[
            jax.ShapeDtypeStruct((2, NEW_TOK, part), bf16),
            jax.ShapeDtypeStruct((2, NEW_TOK, part), f32),
        ],
        scratch_shapes=[
            pltpu.VMEM((NEW_TOK, 4 * part), bf16),
            pltpu.VMEM((NEW_TOK, units), bf16),
            up,
            up,
            pltpu.VMEM((groups, units, cols), bf16),
            pltpu.SemaphoreType.DMA((8 + groups,)),
        ],
        compiler_params=params(),
        cost_estimate=pl.CostEstimate(flops=8 * 10**9, bytes_accessed=28 << 20, transcendentals=1 << 18),
        name="mlp",
    )(t, at, down_at, both, beyond, gain.reshape(4, 1, part), *weights)


def swap(x, bit, size=4):
    return lax.ppermute(x, "tp", [(i, i ^ bit) for i in range(size)])


def gather_pieces(x):
    across = swap(x, 2)
    beside = swap(x, 1)
    return [x, beside, across, swap(across, 1)]


def ring_order(groups):
    return list(range(0, groups, 2)) + list(range(groups - 1, 0, -2))


def shards(
    tokens,
    attn_gain,
    w_query,
    w_key,
    w_value,
    w_out,
    mlp_gain,
    w_gate,
    w_up,
    w_down,
    k_cache,
    v_cache,
    prefix_len,
):
    groups = lax.axis_size("grp")
    group = lax.axis_index("grp")
    tp = lax.axis_index("tp")
    t = tp.reshape(1)
    ring = ring_order(groups)
    where = [ring.index(g) for g in range(groups)]
    each = groups // 4

    def gather(x):
        return lax.all_gather(x, "grp", axis=0, axis_index_groups=[ring])

    if w_gate.shape[1] == 4 * w_down.shape[1]:
        weights = [gather(pack(w_gate, w_up, w_down))]
        feature_at = jnp.array(where, jnp.int32)
    else:
        weights = [lax.all_gather(w, "grp", axis=0, tiled=True).reshape(4, -1, w.shape[1]) for w in (w_gate, w_up)]
        weights.append(gather(w_down))
        feature_at = jnp.arange(4, dtype=jnp.int32)
    shares = [[where[(d ^ i) * each + c] for i in SHARE_ORDER for c in range(each)] for d in range(4)]
    down_at = jnp.array(shares, jnp.int32)[tp]

    own_len = lax.dynamic_index_in_dim(prefix_len, group, keepdims=False)
    half = HD // 2
    inverse = rope_base ** (-2.0 * jnp.arange(half, dtype=f32) / HD)
    positions = own_len + jnp.arange(NEW_TOK, dtype=jnp.int32)
    angles = inverse[:, None] * positions.astype(f32)[None, :]
    token_pieces = gather_pieces(tokens)
    query, key_new, value_new = project(
        t, token_pieces, attn_gain, w_query, w_key, w_value, jnp.cos(angles), jnp.sin(angles)
    )
    new = jnp.concatenate([key_new, value_new], axis=1)

    def turn(x, by):
        return lax.ppermute(x, "grp", [(g, (g + 2 * by) % groups) for g in range(groups)])

    def cross(x):
        return lax.ppermute(x, "grp", [(g, g ^ 1) for g in range(groups)])

    if groups == 8:
        pairs = groups // 2
        calls = [
            [r for k in range(pairs) for r in ((g - 2 * k) % groups, ((g - 2 * k) % groups) ^ 1)] + [g]
            for g in range(groups)
        ]
        plan = jnp.array(calls, jnp.int32)[group]

        own = [query]
        for k in range(1, pairs - 1):
            own.append(turn(own[-1], 1))
        own.append(turn(query, -1))
        other = [cross(x) for x in own]
        other[1], own[-1] = lax.optimization_barrier((other[1], own[-1]))
        copied = ()

        def call(k, crossed):
            nonlocal copied
            fresh = () if k or crossed else (key_new, value_new)
            source = other[k] if crossed else own[k]
            out, *copied = attend(2 * k + crossed, plan, prefix_len, source, k_cache, v_cache, fresh, copied)
            return out

        def merged(k, kept, given, following):
            both, following[0][following[1]] = lax.optimization_barrier((pair(kept, given), following[0][following[1]]))
            return turn(both, -k)

        parts = [call(0, 0)]
        kept = call(1, 0)
        given = cross(call(1, 1))
        for k in range(2, pairs):
            later = cross(call(k, 1))
            parts.append(merged(k - 1, kept, given, (own, k)))
            kept, given = call(k, 0), later
        parts.append(merged(pairs - 1, kept, given, (other, 0)))
        parts.append(cross(call(0, 1)))
    else:
        every = lax.all_gather(query, "grp", axis=0)
        out = attend_all(group.reshape(1), prefix_len, every, k_cache, v_cache)
        back = lax.all_to_all(out, "grp", split_axis=0, concat_axis=0, tiled=True)
        none = jnp.zeros((1,), jnp.int32)
        no_cache = jnp.zeros((1,) + k_cache.shape[1:], bf16)
        own, *_ = attend(0, jnp.zeros((2,), jnp.int32), none, query, no_cache, no_cache, (key_new, value_new))
        parts = [back[k] for k in range(groups)] + [own]
        news = [gather(new)]
        plan = jnp.array(ring + [0], jnp.int32).at[groups].set(group)
        copied = (k_cache, v_cache)

    send, keep = merge(t, parts, w_out)
    half = (keep + swap(send, 1).astype(f32)).astype(bf16)
    mixed = half.astype(f32) + swap(half[::-1], 2).astype(f32)
    both = (jnp.stack([token_pieces[0], token_pieces[2]]).astype(f32) + mixed).astype(bf16)
    beyond = swap(both, 1)
    first = both[0]
    if groups == 8:
        both, new = lax.optimization_barrier((both, new))
        news = [turn(new, k) for k in range(1, pairs)]
    send, keep = mlp(t, feature_at, down_at, both, beyond, mlp_gain, weights)
    if groups == 8:
        send, keep, *news = lax.optimization_barrier((send, keep, *news))
        news = jnp.stack([new, *news])
        news = [news, cross(news)]
        slots = [0, 2, 4, 6, 1, 3, 5, 7]
        plan = jnp.array([[call[s] for s in slots] + [call[-1]] for call in calls], jnp.int32)[group]
    near = swap(send, 1)
    far = (keep[1] + near[1].astype(f32)).astype(bf16)
    down = keep[0] + near[0].astype(f32) + swap(far, 2).astype(f32)
    result = first.astype(f32) + down
    result, plan = lax.optimization_barrier((result, plan))
    k_next, v_next = append(plan, prefix_len, news, *copied)
    return (result, k_next, v_next)


def solution(mesh):
    placed = (
        P("grp", "tp"),
        P(),
        P(None, "tp"),
        P(None, "tp"),
        P(None, "tp"),
        P("tp", None),
        P(),
        P("grp", "tp"),
        P("grp", "tp"),
        P("tp", "grp"),
        P(None, "grp", "tp"),
        P(None, "grp", "tp"),
        P(),
    )
    return jax.shard_map(
        shards,
        mesh=mesh,
        in_specs=placed,
        out_specs=(P("grp", "tp"), P(None, "grp", "tp"), P(None, "grp", "tp")),
        check_vma=False,
    )
```
